256 devices in a mesh: group: 16 (over y, z_hi), inner: 16 (over z_lo, x, core).
Axes of the slice: x: 4, y: 4, z: 8 (z_hi: 4, z_lo: 2; z = z_hi * 2 + z_lo), core: 2. Of those that a mesh axis runs over, the one named last changes fastest.
Arguments:
- query_rows: bfloat16 [16, 2048, 2560], P('group', 'inner'), may hold values from -6 to 6
- key_rows: bfloat16 [16, 2048, 2560], P('group', 'inner'), may hold values from -6 to 6
- value_rows: bfloat16 [16, 2048, 2560], P('group', 'inner'), may hold values from -6 to 6
- out_rows: bfloat16 [16, 2048, 2560], P('group', 'inner'), may hold values from -6 to 6
- grad_out: bfloat16 [16, 2048, 2560], P('group', 'inner'), may hold values from -6 to 6
- log_sum_exp: float32 [16, 20, 2048], P('group', None, 'inner'), may hold values from 4 to 6
- far_frames: int32 [16, 32, 11], P('group', 'inner'), may hold values from 0 to 15, as said below
- far_blocks: int32 [16, 32, 11], P('group', 'inner'), may hold values from 0 to 7
Outputs:
- grad_query: bfloat16 [16, 2048, 2560], P('group', 'inner')
- grad_key: bfloat16 [16, 2048, 2560], P('group', 'inner')
- grad_value: bfloat16 [16, 2048, 2560], P('group', 'inner')
The draws below stay inside these ranges and needn't reach their ends.
Inputs may be any that keep to these rules, and one draw needn't show every extreme that they name: `far_frames`: for every query tile the 11 listed frames are distinct and each lies 2 or more frames away from the tile's own frame.
All inputs are finite; a program needn't handle non-finite values.
Results may differ from the reference program's by a relative error of at most 0.0054.
Values may be sent and summed in bfloat16 or wider, within the bound.
No kernel may reach another device: no remote copies, remote signals or barrier semaphores. Data moves between devices by JAX's collectives and lax.ppermute only.
A program may use at most 128 MiB of HBM per device.

```python
import math
import jax
import jax.numpy as jnp
from jax import lax

HEADS = 20
FEAT = 2560
TILE = 64
FBLOCK = 8
FRAMES = 16
SPATIAL = 2048
TILES = 32
FAR = 11


def draw_far_frames(key, part):
    key = jax.random.fold_in(key, 11)
    tiles_all = SPATIAL // TILE
    own_frame = jnp.arange(FRAMES, dtype=jnp.int32)[:, None, None]
    other_frame = jnp.arange(FRAMES, dtype=jnp.int32)[None, None, :]
    spacing = jnp.abs(other_frame - own_frame)
    jitter = jax.random.randint(key, (FRAMES, tiles_all, FRAMES), 0, 64, dtype=jnp.int32)
    ranking = jitter + 16 * spacing
    ranking = jnp.where(spacing == FRAMES - 1, -1, ranking)
    ranking = jnp.where(spacing >= 2, ranking, 1 << 20)
    ranking = ranking * FRAMES + other_frame
    ordering = jnp.argsort(ranking, axis=-1, stable=True)
    return ordering[..., :FAR].astype(jnp.int32)


def set_ends(result, key, least, largest):
    index_at = [jax.random.randint(jax.random.fold_in(key, axis), (), 0, length) for axis, length in enumerate(result.shape)]
    longest = result.shape.index(max(result.shape))
    neighbour = index_at[:longest] + [(index_at[longest] + 1) % result.shape[longest]] + index_at[longest + 1:]
    return result.at[tuple(index_at)].set(least).at[tuple(neighbour)].set(largest)


def block_levels(key, extent, cuts, smallest, high):
    factor_of = 1.0
    for dim, shards_of in cuts:
        draws = jax.random.uniform(jax.random.fold_in(jax.random.fold_in(key, 6), dim), (shards_of,), jnp.float32, smallest / len(cuts), high / len(cuts))
        factor_of = factor_of * jnp.repeat(jnp.exp(draws), extent[dim] // shards_of).reshape((-1,) + (1,) * (len(extent) - 1 - dim))
    return factor_of


def noise(rng, shape, deviation, bound, shards=(), kind=jnp.bfloat16):
    drawn = jax.random.normal(rng, shape, jnp.float32) * deviation
    if len(shards) > 0:
        drawn = block_levels(rng, shape, shards, -0.22, 0.18) * drawn
    return jnp.clip(drawn, min=-bound, max=bound).astype(kind)


def setup_inputs(seed: int = 0) -> dict:
    arg_keys = jax.random.split(jax.random.key(seed), 9)
    return {
        "query_rows": noise(arg_keys[0], (FRAMES, SPATIAL, FEAT), 1.0, 6.0, ((0, 16), (1, 16))),
        "key_rows": noise(arg_keys[1], (FRAMES, SPATIAL, FEAT), 1.0, 6.0, ((0, 16), (1, 16))),
        "value_rows": noise(arg_keys[2], (FRAMES, SPATIAL, FEAT), 1.0, 6.0, ((0, 16), (1, 16))),
        "out_rows": noise(arg_keys[3], (FRAMES, SPATIAL, FEAT), 1.0, 6.0, ((0, 16), (1, 16))),
        "grad_out": noise(arg_keys[4], (FRAMES, SPATIAL, FEAT), 1.0, 6.0, ((0, 16), (1, 16))),
        "log_sum_exp": jnp.clip(4.0 + 2.0 * jax.random.uniform(arg_keys[5], (FRAMES, HEADS, SPATIAL), jnp.float32) ** block_levels(arg_keys[5], (FRAMES, HEADS, SPATIAL), ((0, 16), (2, 16)), -0.2, 0.2), 4.0, 6.0),
        "far_frames": draw_far_frames(jax.random.fold_in(arg_keys[8], 71), 0),
        "far_blocks": set_ends(jax.random.randint(arg_keys[7], (FRAMES, TILES, FAR), 0, TILE // FBLOCK), jax.random.fold_in(arg_keys[7], 1), 0, (TILE // FBLOCK) - 1).astype(jnp.int32),
    }


def to_heads(row_data, head_count):
    return row_data.reshape(row_data.shape[0], row_data.shape[1], head_count, row_data.shape[2] // head_count).astype(jnp.float32)

def rounded(tensor):
    return lax.optimization_barrier(tensor.astype(jnp.bfloat16)).astype(jnp.float32)

def merge_heads(tensor):
    return tensor.reshape(tensor.shape[0], tensor.shape[1], tensor.shape[2] * tensor.shape[3])

def pair_terms(query_tiles, grad_tiles, log_tiles, delta_tiles, key_window, value_window, window_mask):
    head_count = log_tiles.shape[1]
    head_size = query_tiles.shape[2] // head_count
    score_scale = 1.0 / math.sqrt(head_size)
    query_heads = to_heads(query_tiles, head_count)
    grad_heads = to_heads(grad_tiles, head_count)
    key_heads = to_heads(key_window, head_count)
    value_heads = to_heads(value_window, head_count)
    scores = jnp.einsum('bqhd,bkhd->bhqk', query_heads, key_heads)
    weights = jnp.exp(scores * score_scale - log_tiles[..., None]) * window_mask[:, None]
    grad_weights = jnp.einsum('bqhd,bkhd->bhqk', grad_heads, value_heads)
    grad_scores = rounded(weights * (grad_weights - delta_tiles[..., None]))
    weights_low = rounded(weights)
    query_part = score_scale * jnp.einsum('bhqk,bkhd->bqhd', grad_scores, key_heads)
    key_part = score_scale * jnp.einsum('bhqk,bqhd->bkhd', grad_scores, query_heads)
    value_part = jnp.einsum('bhqk,bqhd->bkhd', weights_low, grad_heads)
    return (merge_heads(query_part), merge_heads(key_part), merge_heads(value_part))

def build_mask(tile_ids, tiles_total, has_prev, has_next, tile_rows):
    window_slots = jnp.arange(5 * tile_rows, dtype=jnp.int32)
    positions = jnp.arange(tile_rows, dtype=jnp.int32)
    tile_step = window_slots // tile_rows
    offsets = (tile_step - 1) * tile_rows + window_slots % tile_rows
    inside_band = jnp.abs(offsets[:, None] - positions[None, :]) <= tile_rows
    tile_at = tile_ids[:, None] + tile_step[None, :] - 1
    inside_grid = (tile_at >= 0) & (tile_at < tiles_total)
    same_part = (window_slots < 3 * tile_rows)[None, :, None] & inside_band[None] & inside_grid[:, :, None]
    earlier = (window_slots >= 3 * tile_rows) & (window_slots < 4 * tile_rows) & has_prev
    later_slots = (window_slots >= 4 * tile_rows) & has_next
    return (same_part | (earlier | later_slots)[None, :, None]).astype(jnp.float32)

def reference(query_rows, key_rows, value_rows, out_rows, grad_out, log_sum_exp, far_frames, far_blocks):
    frames, spatial, feature = query_rows.shape
    head_count = log_sum_exp.shape[1]
    tiles_all = spatial // TILE
    sub_count = TILE // FBLOCK
    far_count = far_frames.shape[2]
    delta_all = jnp.einsum('fshd,fshd->fhs', to_heads(grad_out, head_count), to_heads(out_rows, head_count))
    tile_ids = jnp.arange(tiles_all, dtype=jnp.int32)

    def tiles_of(row_data, frame_now):
        return lax.dynamic_index_in_dim(row_data, frame_now, 0, keepdims=False).reshape(tiles_all, TILE, feature)

    def stats_of(stat_rows, frame_now):
        picked = lax.dynamic_index_in_dim(stat_rows, frame_now, 0, keepdims=False)
        return picked.reshape(head_count, tiles_all, TILE).transpose(1, 0, 2)
    key_blocks = key_rows.reshape(frames, tiles_all, sub_count, FBLOCK, feature)
    value_blocks = value_rows.reshape(frames, tiles_all, sub_count, FBLOCK, feature)

    def far_frame(frame_now):
        frames_here = lax.dynamic_index_in_dim(far_frames, frame_now, 0, keepdims=False)
        blocks_here = lax.dynamic_index_in_dim(far_blocks, frame_now, 0, keepdims=False)
        far_keys = key_blocks[frames_here, tile_ids[:, None], blocks_here].reshape(tiles_all, far_count * FBLOCK, feature)
        far_values = value_blocks[frames_here, tile_ids[:, None], blocks_here].reshape(tiles_all, far_count * FBLOCK, feature)
        all_ones = jnp.ones((tiles_all, TILE, far_count * FBLOCK), jnp.float32)
        query_part, key_part, value_part = pair_terms(tiles_of(query_rows, frame_now), tiles_of(grad_out, frame_now), stats_of(log_sum_exp, frame_now), stats_of(delta_all, frame_now), far_keys, far_values, all_ones)
        return (query_part.reshape(spatial, feature), key_part.astype(jnp.bfloat16), value_part.astype(jnp.bfloat16))
    far_query, far_key, far_value = lax.map(far_frame, jnp.arange(frames, dtype=jnp.int32))
    index_tiles = tile_ids[None, :, None]

    def scatter_far(part_rows):
        block_terms = part_rows.astype(jnp.float32).reshape(frames, tiles_all, far_count, FBLOCK, feature)
        running = jnp.zeros((frames, tiles_all, sub_count, FBLOCK, feature), jnp.float32)
        running = running.at[far_frames, index_tiles, far_blocks].add(block_terms)
        return running.reshape(frames, spatial, feature)
    far_key_sum = scatter_far(far_key)
    far_value_sum = scatter_far(far_value)
    key_framed = jnp.pad(key_rows, ((1, 1), (0, 0), (0, 0)))
    value_framed = jnp.pad(value_rows, ((1, 1), (0, 0), (0, 0)))

    def near_window(framed, frame_now):
        centre = lax.dynamic_index_in_dim(framed, frame_now + 1, 0, keepdims=False)
        padded = jnp.pad(centre, ((TILE, TILE), (0, 0))).reshape(tiles_all + 2, TILE, feature)
        before = lax.dynamic_index_in_dim(framed, frame_now, 0, keepdims=False).reshape(tiles_all, TILE, feature)
        after_frame = lax.dynamic_index_in_dim(framed, frame_now + 2, 0, keepdims=False).reshape(tiles_all, TILE, feature)
        pieces = [padded[0:tiles_all], padded[1:tiles_all + 1], padded[2:tiles_all + 2], before, after_frame]
        return jnp.concatenate(pieces, axis=1)
    zero_tile = jnp.zeros((1, TILE, feature), jnp.float32)

    def fold(grad_rows):
        lower_part = grad_rows[:, 0:TILE]
        middle = grad_rows[:, TILE:2 * TILE]
        upper_part = grad_rows[:, 2 * TILE:3 * TILE]
        same_part = middle + jnp.concatenate([lower_part[1:], zero_tile]) + jnp.concatenate([zero_tile, upper_part[:-1]])
        earlier = grad_rows[:, 3 * TILE:4 * TILE]
        later_frame = grad_rows[:, 4 * TILE:]
        return (same_part.reshape(spatial, feature), earlier.reshape(spatial, feature), later_frame.reshape(spatial, feature))

    def step(held_sums, frame_now):
        prev_key, prev_value, cur_key, cur_value = held_sums
        pair_mask = build_mask(tile_ids, tiles_all, frame_now > 0, frame_now < frames - 1, TILE)
        near_query, near_key, near_value = pair_terms(tiles_of(query_rows, frame_now), tiles_of(grad_out, frame_now), stats_of(log_sum_exp, frame_now), stats_of(delta_all, frame_now), near_window(key_framed, frame_now), near_window(value_framed, frame_now), jnp.transpose(pair_mask, (0, 2, 1)))
        same_key, earlier_key, later_key = fold(near_key)
        same_value, earlier_value, later_value = fold(near_value)
        next_frame = jnp.minimum(frame_now + 1, frames - 1)
        query_out = near_query.reshape(spatial, feature) + lax.dynamic_index_in_dim(far_query, frame_now, 0, keepdims=False)
        emitted = (query_out.astype(jnp.bfloat16), (prev_key + earlier_key).astype(jnp.bfloat16), (prev_value + earlier_value).astype(jnp.bfloat16))
        held_next = (cur_key + same_key, cur_value + same_value, lax.dynamic_index_in_dim(far_key_sum, next_frame, 0, keepdims=False) + later_key, lax.dynamic_index_in_dim(far_value_sum, next_frame, 0, keepdims=False) + later_value)
        return (held_next, emitted)
    zero_frame = jnp.zeros((spatial, feature), jnp.float32)
    initial = (zero_frame, zero_frame, far_key_sum[0], far_value_sum[0])
    closing, outputs = lax.scan(step, initial, jnp.arange(frames, dtype=jnp.int32))
    grad_query = outputs[0]
    grad_key = jnp.concatenate([outputs[1][1:], closing[0].astype(jnp.bfloat16)[None]], axis=0)
    grad_value = jnp.concatenate([outputs[2][1:], closing[1].astype(jnp.bfloat16)[None]], axis=0)
    return (grad_query, grad_key, grad_value)
```

```python
import functools
import math

import jax
import jax.numpy as jnp
from jax import lax
from jax.experimental import pallas as pl
from jax.experimental.pallas import tpu as pltpu
from jax.sharding import PartitionSpec as P

BF = jnp.bfloat16
F32 = jnp.float32
HEAD = 128
TILE = 64
HALF = 32
BLOCK = 8
GROUP = 16
POS = 128
LOG2E = math.log2(math.e)
SCALE = 1.0 / math.sqrt(HEAD)
BIG = 1e30

Q0, K0, V0, G0 = 0, 128, 256, 384
EK0, EV0, EQ0, EG0 = 512, 576, 640, 672
ST0, ROWS_IN = 704, 720
RQ0, RK0, RV0, REK0, REV0, REQ0, ROWS_OUT = 0, 128, 256, 384, 448, 512, 544


def nt(a, b):
    return lax.dot_general(a, b, (((1,), (1,)), ((), ())), preferred_element_type=F32)


def nn(a, b):
    return jnp.dot(a, b, preferred_element_type=F32)


def cols(h):
    return pl.ds(h * HEAD, HEAD)


def three_terms(x):
    hi = x.astype(BF).astype(F32)
    mid = (x - hi).astype(BF).astype(F32)
    low = ((x - hi) - mid).astype(BF).astype(F32)
    return hi, mid, low


def pack_kernel(
    frame_ref, frames_ref, blocks_ref, q_ref, k_ref, v_ref, o_ref, g_ref, lse_ref,
    send_ref, delta_ref, low_ref, high_ref,
):
    heads = lse_ref.shape[0]
    far = frames_ref.shape[1]
    frame = frame_ref[0]
    ones = jnp.ones((8, HEAD), BF)
    for h in range(heads):
        prod = g_ref[:, cols(h)].astype(F32) * o_ref[:, cols(h)].astype(F32)
        hi = prod.astype(BF)
        lo = (prod - hi.astype(F32)).astype(BF)
        row = nt(ones, hi) + nt(ones, lo)
        delta_ref[h : h + 1, :] = row[0:1, :]
    code = lax.broadcasted_iota(jnp.int32, (1, HEAD), 1)
    code_frame = code // BLOCK
    masks = []
    for t in range(POS // TILE):
        hit = jnp.abs(code_frame - frame) == 1
        for j in range(far):
            hit = hit | (code == frames_ref[t, j] * BLOCK + blocks_ref[t, j])
        masks.append(hit.astype(F32))
    sub = lax.broadcasted_iota(jnp.int32, (16, HEAD), 0)
    lane = lax.broadcasted_iota(jnp.int32, (16, HEAD), 1)
    place = (frame % 4) * HALF
    for d in range(GROUP):
        he, te, half = GROUP + d // 4, (d // 2) % 2, d % 2
        send_ref[d, Q0 : Q0 + POS, :] = q_ref[:, cols(d)]
        send_ref[d, K0 : K0 + POS, :] = k_ref[:, cols(d)]
        send_ref[d, V0 : V0 + POS, :] = v_ref[:, cols(d)]
        send_ref[d, G0 : G0 + POS, :] = g_ref[:, cols(d)]
        rows = slice(te * TILE, te * TILE + TILE)
        part = slice(te * TILE + half * HALF, te * TILE + half * HALF + HALF)
        send_ref[d, EK0 : EK0 + TILE, :] = k_ref[rows, cols(he)]
        send_ref[d, EV0 : EV0 + TILE, :] = v_ref[rows, cols(he)]
        send_ref[d, EQ0 : EQ0 + HALF, :] = q_ref[part, cols(he)]
        send_ref[d, EG0 : EG0 + HALF, :] = g_ref[part, cols(he)]
        main = three_terms(lse_ref[d : d + 1, :]) + three_terms(delta_ref[d : d + 1, :])
        extra = three_terms(lse_ref[he : he + 1, :]) + three_terms(delta_ref[he : he + 1, :])
        mine = jnp.zeros((16, HEAD), F32)
        for i in range(6):
            mine = jnp.where(sub == i, main[i], mine)
        theirs = jnp.zeros((16, HEAD), F32)
        for i in range(6):
            theirs = jnp.where(sub == 6 + i, extra[i], theirs)
        start = te * TILE + half * HALF
        theirs = pltpu.roll(theirs, lax.rem(place + (HEAD - start), HEAD), 1)
        inside = (lane >= place) & (lane < place + HALF)
        both = jnp.where(inside, theirs, 0.0) + mine
        for t in range(2):
            both = jnp.where(sub == 12 + t, masks[t], both)
        send_ref[d, ST0:ROWS_IN, :] = both.astype(BF)
    low_ref[0] = k_ref[0:TILE, :]
    low_ref[1] = v_ref[0:TILE, :]
    high_ref[0] = k_ref[POS - TILE : POS, :]
    high_ref[1] = v_ref[POS - TILE : POS, :]


def own_kernel(
    side_ref, q_ref, k_ref, v_ref, g_ref, before_ref, after_ref, lse_ref, delta_ref,
    dq_ref, dk_ref, dv_ref, low_ref, high_ref,
):
    step = pl.program_id(0)
    per_step = q_ref.shape[1] // HEAD
    width = POS + 2 * TILE
    key = lax.broadcasted_iota(jnp.int32, (width, POS), 0)
    query = lax.broadcasted_iota(jnp.int32, (width, POS), 1)
    first = jnp.where(side_ref[0] > 0, 0, TILE)
    last = jnp.where(side_ref[0] < side_ref[1] - 1, width, width - TILE)
    inside = (key >= query) & (key <= query + 2 * TILE) & (key >= first) & (key < last)
    for j in range(per_step):
        h = step * per_step + j
        q = q_ref[:, cols(j)]
        g = g_ref[:, cols(j)]
        k = jnp.concatenate([before_ref[0, :, cols(j)], k_ref[:, cols(j)], after_ref[0, :, cols(j)]], 0)
        v = jnp.concatenate([before_ref[1, :, cols(j)], v_ref[:, cols(j)], after_ref[1, :, cols(j)]], 0)
        lse = lse_ref[pl.ds(h, 1), :]
        delta = delta_ref[pl.ds(h, 1), :]
        p = jnp.exp2(nt(k, q) * (SCALE * LOG2E) - lse * LOG2E)
        p = jnp.where(inside, p, 0.0)
        ds = (p * (nt(v, g) - delta)).astype(BF)
        dv = nn(p.astype(BF), g)
        dk = nn(ds, q) * SCALE
        dq = lax.dot_general(ds, k, (((0,), (0,)), ((), ())), preferred_element_type=F32)
        dq_ref[:, cols(j)] = dq * SCALE
        dk_ref[:, cols(j)] = dk[TILE : TILE + POS]
        dv_ref[:, cols(j)] = dv[TILE : TILE + POS]
        low_ref[0, :, cols(j)] = dk[0:TILE].astype(BF)
        low_ref[1, :, cols(j)] = dv[0:TILE].astype(BF)
        high_ref[0, :, cols(j)] = dk[TILE + POS :].astype(BF)
        high_ref[1, :, cols(j)] = dv[TILE + POS :].astype(BF)


def cross_kernel(in_ref, out_ref, kx_ref, kt_ref, dk_ref, dv_ref, row_ref):
    keys = GROUP * TILE
    chunk = 256
    stats = in_ref[:, ST0:ROWS_IN, :].astype(F32)
    lane = lax.broadcasted_iota(jnp.int32, (1, HEAD), 1)
    spread = (
        lax.broadcasted_iota(jnp.int32, (keys, HEAD), 0) // BLOCK
        == lax.broadcasted_iota(jnp.int32, (keys, HEAD), 1)
    ).astype(BF)
    for unit in range(3):
        main = unit < 2
        if main:
            span = TILE
            q_at, k_at = Q0 + unit * TILE, K0 + unit * TILE
            v_at, g_at = V0 + unit * TILE, G0 + unit * TILE
            dq_at, dk_at, dv_at = RQ0 + unit * TILE, RK0 + unit * TILE, RV0 + unit * TILE
            mask = in_ref[:, ST0 + 12 + unit, :]
        else:
            span = HALF
            q_at, k_at, v_at, g_at = EQ0, EK0, EV0, EG0
            dq_at, dk_at, dv_at = REQ0, REK0, REV0
            second = (lax.axis_index("group") // 2) % 2
            mask = jnp.where(second == 1, in_ref[:, ST0 + 13, :], in_ref[:, ST0 + 12, :])
        per = HEAD // span
        base = 0 if main else 6
        for s in range(2):
            at = base + 3 * s
            full = (stats[:, at, :] + stats[:, at + 1, :]) + stats[:, at + 2, :]
            if main:
                turned = pltpu.roll(full, TILE, 1)
                left, right = (full, turned) if unit == 0 else (turned, full)
                for i in range(GROUP // per):
                    row_ref[s, i : i + 1, :] = jnp.where(
                        lane < TILE, left[2 * i : 2 * i + 1], right[2 * i + 1 : 2 * i + 2]
                    )
            else:
                for i in range(GROUP // per):
                    row_ref[s, i : i + 1, :] = (full[4 * i : 4 * i + 1] + full[4 * i + 1 : 4 * i + 2]) + (
                        full[4 * i + 2 : 4 * i + 3] + full[4 * i + 3 : 4 * i + 4]
                    )
        k = in_ref[:, k_at : k_at + TILE, :].reshape(keys, HEAD)
        v = in_ref[:, v_at : v_at + TILE, :].reshape(keys, HEAD)
        padded = jnp.concatenate([mask.astype(F32), jnp.zeros((HEAD - GROUP, HEAD), F32)], 0)
        kx_ref[:, 0:HEAD] = k
        kx_ref[:, HEAD:] = ((nt(spread, padded.astype(BF)) - 1.0) * BIG).astype(BF)
        kt_ref[...] = k.astype(F32).T.astype(BF)
        dk_ref[...] = jnp.zeros_like(dk_ref)
        dv_ref[...] = jnp.zeros_like(dv_ref)
        count = chunk // span
        query = lax.broadcasted_iota(jnp.int32, (chunk, HEAD), 0) // span
        column = lax.broadcasted_iota(jnp.int32, (chunk, HEAD), 1)

        def one_chunk(c, carry):
            frames = pl.ds(c * count, count)
            q = in_ref[frames, q_at : q_at + span, :].reshape(chunk, HEAD)
            g = in_ref[frames, g_at : g_at + span, :].reshape(chunk, HEAD)
            choose = (column == query + c * count).astype(F32).astype(BF)
            qx = jnp.concatenate([q, choose], 1)
            lse = jnp.concatenate([row_ref[0, pl.ds(2 * c + i, 1), :] for i in range(2)], 1)
            delta = jnp.concatenate([row_ref[1, pl.ds(2 * c + i, 1), :] for i in range(2)], 1)
            p = jnp.exp2(nt(kx_ref[...], qx) * (SCALE * LOG2E) - lse * LOG2E)
            ds = (p * (nt(v, g) - delta)).astype(BF)
            dv_ref[...] += nn(p.astype(BF), g)
            dk_ref[...] += nn(ds, q)
            dq = (nn(kt_ref[...], ds) * SCALE).T.astype(BF)
            out_ref[frames, dq_at : dq_at + span, :] = dq.reshape(count, span, HEAD)
            return carry

        lax.fori_loop(0, GROUP * span // chunk, one_chunk, 0)
        out_ref[:, dk_at : dk_at + TILE, :] = (dk_ref[...] * SCALE).astype(BF).reshape(GROUP, TILE, HEAD)
        out_ref[:, dv_at : dv_at + TILE, :] = dv_ref[...].astype(BF).reshape(GROUP, TILE, HEAD)


def join_kernel(
    back_ref, dq_in, dk_in, dv_in, left_ref, right_ref, dq_ref, dk_ref, dv_ref
):
    step = pl.program_id(0)
    per_step = dq_ref.shape[1] // HEAD

    def finish(j, dq, dk, dv):
        dq_ref[:, cols(j)] = (dq_in[:, cols(j)] + dq).astype(BF)
        for i, (own, ref, more) in enumerate(((dk_in, dk_ref, dk), (dv_in, dv_ref, dv))):
            total = own[:, cols(j)] + more
            side = jnp.concatenate([left_ref[i, :, cols(j)], right_ref[i, :, cols(j)]], 0)
            ref[:, cols(j)] = (total + side.astype(F32)).astype(BF)

    @pl.when(step < 4)
    def _():
        for j in range(per_step):
            d = step * per_step + j
            finish(
                j,
                back_ref[d, RQ0 : RQ0 + POS, :].astype(F32),
                back_ref[d, RK0 : RK0 + POS, :].astype(F32),
                back_ref[d, RV0 : RV0 + POS, :].astype(F32),
            )

    @pl.when(step == 4)
    def _():
        for j in range(per_step):
            four = range(4 * j, 4 * j + 4)
            dq = jnp.concatenate([back_ref[d, REQ0:ROWS_OUT, :].astype(F32) for d in four], 0)
            sums = []
            for at in (REK0, REV0):
                part = [back_ref[d, at : at + TILE, :].astype(F32) for d in four]
                sums.append(jnp.concatenate([part[0] + part[1], part[2] + part[3]], 0))
            finish(j, dq, sums[0], sums[1])


VMEM = pl.BlockSpec(memory_space=pltpu.VMEM)
SMEM = pl.BlockSpec(memory_space=pltpu.SMEM)
ROOM = 48 * 1024 * 1024


def body(query_rows, key_rows, value_rows, out_rows, grad_out, log_sum_exp, far_frames, far_blocks):
    q, k, v, o, g = (a[0] for a in (query_rows, key_rows, value_rows, out_rows, grad_out))
    lse = log_sum_exp[0]
    feature = q.shape[1]
    heads = lse.shape[0]
    inner = lax.axis_size("inner")
    inner_at = lax.axis_index("inner")
    frame = lax.axis_index("group").reshape(1).astype(jnp.int32)
    sides = jnp.stack([inner_at, jnp.full((), inner, inner_at.dtype)]).astype(jnp.int32)
    halo = jax.ShapeDtypeStruct((2, TILE, feature), BF)

    send, delta, first_rows, last_rows = pl.pallas_call(
        pack_kernel,
        out_shape=(
            jax.ShapeDtypeStruct((GROUP, ROWS_IN, HEAD), BF),
            jax.ShapeDtypeStruct((heads, POS), F32),
            halo,
            halo,
        ),
        in_specs=[SMEM] * 3 + [VMEM] * 6,
        out_specs=[VMEM] * 4,
        compiler_params=pltpu.CompilerParams(vmem_limit_bytes=ROOM),
        name="pack",
    )(frame, far_frames[0], far_blocks[0], q, k, v, o, g, lse)

    arrived = lax.all_to_all(send, "group", 0, 0, tiled=True)

    up = [(i, i + 1) for i in range(inner - 1)]
    down = [(i + 1, i) for i in range(inner - 1)]
    before = lax.ppermute(last_rows, "inner", up)
    after = lax.ppermute(first_rows, "inner", down)

    wide = 4 * HEAD
    rows = pl.BlockSpec((POS, wide), lambda i: (0, i))
    edge = pl.BlockSpec((2, TILE, wide), lambda i: (0, 0, i))
    whole = pl.BlockSpec((heads, POS), lambda i: (0, 0))
    own_shape = jax.ShapeDtypeStruct((POS, feature), F32)
    dq_own, dk_own, dv_own, to_low, to_high = pl.pallas_call(
        own_kernel,
        grid=(feature // wide,),
        out_shape=(own_shape, own_shape, own_shape, halo, halo),
        in_specs=[SMEM, rows, rows, rows, rows, edge, edge, whole, whole],
        out_specs=[rows, rows, rows, edge, edge],
        compiler_params=pltpu.CompilerParams(vmem_limit_bytes=ROOM),
        name="own",
    )(sides, q, k, v, g, before, after, lse, delta)
    from_right = lax.ppermute(to_low, "inner", down)
    from_left = lax.ppermute(to_high, "inner", up)

    keys = GROUP * TILE
    back = pl.pallas_call(
        cross_kernel,
        out_shape=jax.ShapeDtypeStruct((GROUP, ROWS_OUT, HEAD), BF),
        in_specs=[VMEM],
        out_specs=VMEM,
        scratch_shapes=[
            pltpu.VMEM((keys, 2 * HEAD), BF),
            pltpu.VMEM((HEAD, keys), BF),
            pltpu.VMEM((keys, HEAD), F32),
            pltpu.VMEM((keys, HEAD), F32),
            pltpu.VMEM((2, 8, HEAD), F32),
        ],
        compiler_params=pltpu.CompilerParams(vmem_limit_bytes=ROOM),
        name="cross",
    )(arrived)
    returned = lax.all_to_all(back, "group", 0, 0, tiled=True)

    out_shape = jax.ShapeDtypeStruct((POS, feature), BF)
    outs = pl.pallas_call(
        join_kernel,
        grid=(feature // wide,),
        out_shape=(out_shape,) * 3,
        in_specs=[VMEM, rows, rows, rows, edge, edge],
        out_specs=[rows] * 3,
        compiler_params=pltpu.CompilerParams(vmem_limit_bytes=ROOM),
        name="join",
    )(returned, dq_own, dk_own, dv_own, from_left, from_right)
    return tuple(a[None] for a in outs)


def solution(mesh):
    shard = P("group", "inner", None)
    return jax.shard_map(
        body,
        mesh=mesh,
        in_specs=(shard,) * 5 + (P("group", None, "inner"), shard, shard),
        out_specs=(shard,) * 3,
        check_vma=False,
    )
```

```python
import functools
import math

import jax
import jax.numpy as jnp
from jax import lax
from jax.experimental import pallas as pl
from jax.experimental.pallas import tpu as pltpu
from jax.sharding import PartitionSpec as P

BF = jnp.bfloat16
F32 = jnp.float32
HEAD = 128
TILE = 64
HALF = 32
BLOCK = 8
GROUP = 16
SIDE = 4
POS = 128
WIDE = SIDE * HEAD
LOG2E = math.log2(math.e)
SCALE = 1.0 / math.sqrt(HEAD)
BIG = 1e30

BQ, BK, BV, BG, BS, ROWS_B = 0, 128, 256, 384, 512, 528
BACK_B = 384
AK, AV, AQ, AG, AS, ROWS_A = 0, 64, 128, 160, 192, 208
RK, RV, RQ, ROWS_R = 0, 64, 128, 160


def nt(a, b):
    return lax.dot_general(a, b, (((1,), (1,)), ((), ())), preferred_element_type=F32)


def nn(a, b):
    return jnp.dot(a, b, preferred_element_type=F32)


def cols(h):
    return pl.ds(h * HEAD, HEAD)


def three_terms(x):
    hi = x.astype(BF).astype(F32)
    mid = (x - hi).astype(BF).astype(F32)
    low = ((x - hi) - mid).astype(BF).astype(F32)
    return hi, mid, low


class Copies:
    def __init__(self, sems):
        self.sems, self.used, self.open = sems, 0, {}

    def start(self, key, source, target):
        copy = pltpu.make_async_copy(source, target, self.sems.at[self.used])
        copy.start()
        self.used += 1
        self.open.setdefault(key, []).append(copy)

    def wait(self, key):
        for copy in self.open.pop(key, []):
            copy.wait()

    def wait_all(self):
        for key in list(self.open):
            self.wait(key)


class Copies:
    def __init__(self, sems):
        self.sems, self.used, self.open = sems, 0, {}

    def start(self, key, source, target):
        copy = pltpu.make_async_copy(source, target, self.sems.at[self.used])
        copy.start()
        self.used += 1
        self.open.setdefault(key, []).append(copy)

    def wait(self, key):
        for copy in self.open.pop(key, []):
            copy.wait()

    def wait_all(self):
        for key in list(self.open):
            self.wait(key)


def deltas(grads, outs):
    ones = jnp.ones((8, HEAD), BF)
    prod = jnp.concatenate([g.astype(F32) * o.astype(F32) for g, o in zip(grads, outs)], 0)
    hi = prod.astype(BF)
    lo = (prod - hi.astype(F32)).astype(BF)
    sums = nt(ones, hi) + nt(ones, lo)
    return [sums[0:1, j * HEAD : j * HEAD + HEAD] for j in range(len(grads))]


def pair_masks(frame, frames_ref, blocks_ref):
    code = lax.broadcasted_iota(jnp.int32, (1, HEAD), 1)
    masks = []
    for t in range(POS // TILE):
        hit = jnp.abs(code // BLOCK - frame) == 1
        for j in range(frames_ref.shape[1]):
            hit = hit | (code == frames_ref[t, j] * BLOCK + blocks_ref[t, j])
        masks.append(hit.astype(F32))
    return masks


def stat_rows(lse, delta, masks):
    sub = lax.broadcasted_iota(jnp.int32, (16, HEAD), 0)
    rows = jnp.zeros((16, HEAD), F32)
    for i, term in enumerate(list(three_terms(lse) + three_terms(delta)) + masks):
        rows = jnp.where(sub == i, term, rows)
    return rows


def pack_a_kernel(
    place_ref, frames_ref, blocks_ref, lse_ref, q_hbm, k_hbm, v_hbm, o_hbm, g_hbm,
    z0_hbm, z1_hbm, z2_hbm, z3_hbm, low_hbm, high_hbm,
    q_all, k_all, v_all, o_all, g_all, send_ref, edge_ref, sems,
):
    copies = Copies(sems)
    at = slice(SIDE * WIDE, SIDE * WIDE + WIDE)
    for source, target in zip((g_hbm, o_hbm, q_hbm, k_hbm, v_hbm), (g_all, o_all, q_all, k_all, v_all)):
        copies.start("in", source.at[:, at], target)
    for i, source in enumerate((k_hbm, v_hbm)):
        copies.start("edge", source.at[0:TILE, :], edge_ref.at[0, i])
        copies.start("edge", source.at[POS - TILE : POS, :], edge_ref.at[1, i])
    masks = pair_masks(place_ref[0] * SIDE + place_ref[1], frames_ref, blocks_ref)
    copies.wait("in")
    rows = deltas([g_all[:, cols(j)] for j in range(SIDE)], [o_all[:, cols(j)] for j in range(SIDE)])
    for j in range(SIDE):
        send_ref[j, BQ : BQ + POS, :] = q_all[:, cols(j)]
        send_ref[j, BK : BK + POS, :] = k_all[:, cols(j)]
        send_ref[j, BV : BV + POS, :] = v_all[:, cols(j)]
        send_ref[j, BG : BG + POS, :] = g_all[:, cols(j)]
        send_ref[j, BS:ROWS_B, :] = stat_rows(lse_ref[GROUP + j], rows[j], masks).astype(BF)
    for dz, out in enumerate((z0_hbm, z1_hbm, z2_hbm, z3_hbm)):
        copies.start("out", send_ref.at[lax.rem(place_ref[1] + dz, SIDE)], out)
    copies.wait("edge")
    copies.start("out", edge_ref.at[0], low_hbm)
    copies.start("out", edge_ref.at[1], high_hbm)
    copies.wait_all()


def pack_b_kernel(
    place_ref, frames_ref, blocks_ref, lse_ref, q_hbm, k_hbm, v_hbm, o_hbm, g_hbm, send_hbm,
    q_all, k_all, v_all, o_all, g_all, send_ref, sems,
):
    copies = Copies(sems)
    pairs = ((g_hbm, g_all), (o_hbm, o_all), (q_hbm, q_all), (k_hbm, k_all), (v_hbm, v_all))
    for block in range(SIDE):
        at = slice(block * WIDE, block * WIDE + WIDE)
        for source, target in pairs:
            copies.start(block, source.at[:, at], target.at[:, at])
    masks = pair_masks(place_ref[0] * SIDE + place_ref[1], frames_ref, blocks_ref)
    for block in range(SIDE):
        copies.wait(block)
        heads = [block * SIDE + j for j in range(SIDE)]
        rows = deltas([g_all[:, cols(h)] for h in heads], [o_all[:, cols(h)] for h in heads])
        for j, h in enumerate(heads):
            send_ref[h, BQ : BQ + POS, :] = q_all[:, cols(h)]
            send_ref[h, BK : BK + POS, :] = k_all[:, cols(h)]
            send_ref[h, BV : BV + POS, :] = v_all[:, cols(h)]
            send_ref[h, BG : BG + POS, :] = g_all[:, cols(h)]
            send_ref[h, BS:ROWS_B, :] = stat_rows(lse_ref[h], rows[j], masks).astype(BF)
        four = slice(block * SIDE, block * SIDE + SIDE)
        copies.start("out", send_ref.at[four], send_hbm.at[four])
    copies.wait_all()


def split_kernel(place_ref, *refs):
    ins, outs = refs[:SIDE], refs[SIDE:]
    lane = lax.broadcasted_iota(jnp.int32, (16, HEAD), 1)
    sub = lax.broadcasted_iota(jnp.int32, (16, HEAD), 0)
    for dz, got in enumerate(ins):
        stats = got[BS:ROWS_B, :].astype(F32)
        for dy, out in enumerate(outs):
            y = lax.rem(place_ref[0] + dy, SIDE)
            tile = pl.multiple_of((y // 2) * TILE, TILE)
            half = pl.multiple_of(y * HALF, HALF)
            out[dz, AK : AK + TILE, :] = got[pl.ds(BK + tile, TILE), :]
            out[dz, AV : AV + TILE, :] = got[pl.ds(BV + tile, TILE), :]
            out[dz, AQ : AQ + HALF, :] = got[pl.ds(BQ + half, HALF), :]
            out[dz, AG : AG + HALF, :] = got[pl.ds(BG + half, HALF), :]
            turned = pltpu.roll(stats, lax.rem(dz * HALF + HEAD - half, HEAD), 1)
            inside = (lane >= dz * HALF) & (lane < dz * HALF + HALF)
            kept = jnp.where(sub < 6, jnp.where(inside, turned, 0.0), stats)
            out[dz, AS:ROWS_A, :] = kept.astype(BF)


def own_kernel(
    side_ref, q_ref, k_ref, v_ref, o_ref, g_ref, before_ref, after_ref, lse_ref,
    sums_ref, low_ref, high_ref,
):
    step = pl.program_id(0)
    width = POS + 2 * TILE
    key = lax.broadcasted_iota(jnp.int32, (width, POS), 0)
    query = lax.broadcasted_iota(jnp.int32, (width, POS), 1)
    first = jnp.where(side_ref[0] > 0, 0, TILE)
    last = jnp.where(side_ref[0] < side_ref[1] - 1, width, width - TILE)
    inside = (key >= query) & (key <= query + 2 * TILE) & (key >= first) & (key < last)
    rows = deltas([g_ref[:, cols(j)] for j in range(SIDE)], [o_ref[:, cols(j)] for j in range(SIDE)])
    for j in range(SIDE):
        q = q_ref[:, cols(j)]
        g = g_ref[:, cols(j)]
        k = jnp.concatenate([before_ref[0, :, cols(j)], k_ref[:, cols(j)], after_ref[0, :, cols(j)]], 0)
        v = jnp.concatenate([before_ref[1, :, cols(j)], v_ref[:, cols(j)], after_ref[1, :, cols(j)]], 0)
        lse = lse_ref[step * SIDE + j]
        p = jnp.exp2(nt(k, q) * (SCALE * LOG2E) - lse * LOG2E)
        p = jnp.where(inside, p, 0.0)
        ds = (p * (nt(v, g) - rows[j])).astype(BF)
        dv = nn(p.astype(BF), g)
        dk = nn(ds, q) * SCALE
        dq = lax.dot_general(ds, k, (((0,), (0,)), ((), ())), preferred_element_type=F32)
        sums_ref[0, :, cols(j)] = dq * SCALE
        sums_ref[1, :, cols(j)] = dk[TILE : TILE + POS]
        sums_ref[2, :, cols(j)] = dv[TILE : TILE + POS]
        low_ref[0, :, cols(j)] = dk[0:TILE].astype(BF)
        low_ref[1, :, cols(j)] = dv[0:TILE].astype(BF)
        high_ref[0, :, cols(j)] = dk[TILE + POS :].astype(BF)
        high_ref[1, :, cols(j)] = dv[TILE + POS :].astype(BF)


CHUNK = 512
UNROLL = 2
KEYS = GROUP * TILE


def attend(span, queries, key_code, k, v, mask, rows, kx_ref, kt_ref, dk_ref, dv_ref, row_ref, put_dq):
    for s in range(2):
        row_ref[s] = rows[s]
    lane = lax.broadcasted_iota(jnp.int32, (KEYS, HEAD), 1)
    spread = (key_code == lane).astype(F32).astype(BF)
    padded = jnp.concatenate([mask.astype(F32), jnp.zeros((HEAD - GROUP, HEAD), F32)], 0)
    kx_ref[:, 0:HEAD] = k
    kx_ref[:, HEAD:] = ((nt(spread, padded.astype(BF)) - 1.0) * BIG).astype(BF)
    kt_ref[...] = k.astype(F32).T.astype(BF)
    dk_ref[...] = jnp.zeros_like(dk_ref)
    dv_ref[...] = jnp.zeros_like(dv_ref)
    count = CHUNK // span
    query = lax.broadcasted_iota(jnp.int32, (CHUNK, HEAD), 0) // span
    column = lax.broadcasted_iota(jnp.int32, (CHUNK, HEAD), 1)

    def one_chunk(c, carry):
        frames = pl.ds(c * count, count)
        q, g = queries(frames)
        choose = (column == query + c * count).astype(F32).astype(BF)
        qx = jnp.concatenate([q, choose], 1)
        lanes = CHUNK // HEAD
        lse, delta = (
            jnp.concatenate([row_ref[s, pl.ds(lanes * c + i, 1), :] for i in range(lanes)], 1) for s in range(2)
        )
        p = jnp.exp2(nt(kx_ref[...], qx) * (SCALE * LOG2E) - lse * LOG2E)
        ds = (p * (nt(v, g) - delta)).astype(BF)
        dv_ref[...] += nn(p.astype(BF), g)
        dk_ref[...] += nn(ds, q)
        put_dq(frames, (nn(kt_ref[...], ds) * SCALE).T.astype(BF).reshape(count, span, HEAD))
        return carry

    lax.fori_loop(0, GROUP * span // CHUNK, one_chunk, 0, unroll=UNROLL)


def added(stats, at):
    return (stats[:, at, :] + stats[:, at + 1, :]) + stats[:, at + 2, :]


def stacked(rows):
    rows = rows + [jnp.zeros((8 - len(rows), HEAD), F32)] if len(rows) < 8 else rows
    return jnp.concatenate(rows, 0)


def quarter_kernel(place_ref, *refs):
    ins, outs = refs[:SIDE], refs[SIDE : 2 * SIDE]
    q_ref, g_ref, kx_ref, kt_ref, dk_ref, dv_ref, row_ref = refs[2 * SIDE :]
    y, z = place_ref[0], place_ref[1]
    stats = jnp.concatenate([got[:, AS:ROWS_A, :] for got in ins], 0).astype(F32)
    rows = []
    for s in range(2):
        full = added(stats, 3 * s)
        rows.append(
            stacked(
                [
                    (full[i : i + 1] + full[i + 1 : i + 2]) + (full[i + 2 : i + 3] + full[i + 3 : i + 4])
                    for i in range(0, GROUP, SIDE)
                ]
            )
        )
    mask = jnp.where(y >= 2, stats[:, 7, :], stats[:, 6, :])
    k = jnp.concatenate([got[:, AK : AK + TILE, :] for got in ins], 0)
    v = jnp.concatenate([got[:, AV : AV + TILE, :] for got in ins], 0)
    for i, got in enumerate(ins):
        q_ref[SIDE * i : SIDE * i + SIDE] = got[:, AQ : AQ + HALF, :]
        g_ref[SIDE * i : SIDE * i + SIDE] = got[:, AG : AG + HALF, :]
    row = lax.broadcasted_iota(jnp.int32, (KEYS, HEAD), 0)
    source_y = (y + SIDE - row // (SIDE * TILE)) % SIDE
    source_z = (z + SIDE - (row // TILE) % SIDE) % SIDE
    key_code = (source_y * SIDE + source_z) * BLOCK + (row % TILE) // BLOCK

    def queries(frames):
        return q_ref[frames].reshape(CHUNK, HEAD), g_ref[frames].reshape(CHUNK, HEAD)

    def put_dq(frames, dq):
        q_ref[frames] = dq

    attend(
        HALF, queries, key_code, k.reshape(KEYS, HEAD), v.reshape(KEYS, HEAD), mask, rows,
        kx_ref, kt_ref, dk_ref, dv_ref, row_ref, put_dq,
    )
    span = SIDE * TILE
    for i, out in enumerate(outs):
        dk = (dk_ref[i * span : i * span + span] * SCALE).astype(BF)
        dv = dv_ref[i * span : i * span + span].astype(BF)
        out[:, RK : RK + TILE, :] = dk.reshape(SIDE, TILE, HEAD)
        out[:, RV : RV + TILE, :] = dv.reshape(SIDE, TILE, HEAD)
        out[:, RQ : RQ + HALF, :] = q_ref[SIDE * i : SIDE * i + SIDE]


def merge_kernel(place_ref, *refs):
    ins, outs, sum_ref = refs[:SIDE], refs[SIDE : 2 * SIDE], refs[2 * SIDE]
    sum_ref[...] = jnp.zeros_like(sum_ref)
    for dy, got in enumerate(ins):
        y = lax.rem(place_ref[0] + dy, SIDE)
        tile = pl.multiple_of((y // 2) * TILE, TILE)
        half = pl.multiple_of(y * HALF, HALF)
        for dz, out in enumerate(outs):
            out[pl.ds(BQ + half, HALF), :] = got[dz, RQ:ROWS_R, :]
            sum_ref[dz, 0, pl.ds(tile, TILE), :] += got[dz, RK : RK + TILE, :].astype(F32)
            sum_ref[dz, 1, pl.ds(tile, TILE), :] += got[dz, RV : RV + TILE, :].astype(F32)
    for dz, out in enumerate(outs):
        out[BK : BK + POS, :] = sum_ref[dz, 0].astype(BF)
        out[BV : BV + POS, :] = sum_ref[dz, 1].astype(BF)


def head_kernel(in_hbm, out_hbm, in_ref, out_ref, sems, *scratch):
    copies = Copies(sems)

    def fetch(key, first, count):
        copies.start(key, in_hbm.at[:, first : first + count, :], in_ref.at[:, first : first + count, :])

    fetch("stats", BS, ROWS_B - BS)
    for unit in range(2):
        for at in (BK, BV, BQ, BG):
            fetch(unit, at + unit * TILE, TILE)
    key_code = lax.broadcasted_iota(jnp.int32, (KEYS, HEAD), 0) // BLOCK
    lane = lax.broadcasted_iota(jnp.int32, (1, HEAD), 1)
    copies.wait("stats")
    stats = in_ref[:, BS:ROWS_B, :].astype(F32)
    for unit in range(2):
        at = unit * TILE
        rows = []
        for s in range(2):
            full = added(stats, 3 * s)
            turned = pltpu.roll(full, TILE, 1)
            left, right = (full, turned) if unit == 0 else (turned, full)
            rows.append(
                stacked(
                    [jnp.where(lane < TILE, left[i : i + 1], right[i + 1 : i + 2]) for i in range(0, GROUP, 2)]
                )
            )

        def queries(frames):
            q = in_ref[frames, BQ + at : BQ + at + TILE, :].reshape(CHUNK, HEAD)
            g = in_ref[frames, BG + at : BG + at + TILE, :].reshape(CHUNK, HEAD)
            return q, g

        def put_dq(frames, dq):
            out_ref[frames, BQ + at : BQ + at + TILE, :] = dq

        copies.wait(unit)
        attend(
            TILE, queries, key_code,
            in_ref[:, BK + at : BK + at + TILE, :].reshape(KEYS, HEAD),
            in_ref[:, BV + at : BV + at + TILE, :].reshape(KEYS, HEAD),
            stats[:, 6 + unit, :], rows, *scratch, put_dq,
        )
        dk_ref, dv_ref = scratch[2:4]
        dk = (dk_ref[...] * SCALE).astype(BF).reshape(GROUP, TILE, HEAD)
        out_ref[:, BK + at : BK + at + TILE, :] = dk
        out_ref[:, BV + at : BV + at + TILE, :] = dv_ref[...].astype(BF).reshape(GROUP, TILE, HEAD)
        for first in (BQ + at, BK + at, BV + at):
            part = slice(first, first + TILE)
            copies.start("out", out_ref.at[:, part, :], out_hbm.at[:, part, :])
    copies.wait_all()


def join_kernel(
    place_ref, z0_hbm, z1_hbm, z2_hbm, z3_hbm, b_hbm, sums_in, left_in, right_in, dq_out, dk_out, dv_out,
    a_ref, b_ref, sums_ref, left_ref, right_ref, low_ref, sems,
):
    copies = Copies(sems)
    sets = ((dq_out, BQ), (dk_out, BK), (dv_out, BV))
    order = [SIDE] + list(range(SIDE))
    for block in order:
        at = slice(block * WIDE, block * WIDE + WIDE)
        if block == SIDE:
            for dz, share in enumerate((z0_hbm, z1_hbm, z2_hbm, z3_hbm)):
                copies.start(block, share, a_ref.at[dz])
        else:
            four = slice(SIDE * block, SIDE * block + SIDE)
            copies.start(block, b_hbm.at[four], b_ref.at[four])
        copies.start(block, sums_in.at[:, :, at], sums_ref.at[:, :, at])
        copies.start(block, left_in.at[:, :, at], left_ref.at[:, :, at])
        copies.start(block, right_in.at[:, :, at], right_ref.at[:, :, at])
    for block in order:
        copies.wait(block)
        at = slice(block * WIDE, block * WIDE + WIDE)
        for which, (out, row) in enumerate(sets):
            for j in range(SIDE):
                h = SIDE * block + j
                if block < SIDE:
                    more = b_ref[h, row : row + POS, :].astype(F32)
                else:
                    dz = lax.rem(j + SIDE - place_ref[1], SIDE)
                    more = a_ref[dz, row : row + POS, :].astype(F32)
                if which:
                    edges = [left_ref[which - 1, :, cols(h)], right_ref[which - 1, :, cols(h)]]
                    more = more + jnp.concatenate(edges, 0).astype(F32)
                low_ref[which, :, cols(h)] = (sums_ref[which, :, cols(h)] + more).astype(BF)
            copies.start("out", low_ref.at[which, :, at], out.at[:, at])
    copies.wait_all()


VMEM = pl.BlockSpec(memory_space=pltpu.VMEM)
SMEM = pl.BlockSpec(memory_space=pltpu.SMEM)
ANY = pl.BlockSpec(memory_space=pl.ANY)
MIB = 1024 * 1024


def room(mib):
    return pltpu.CompilerParams(vmem_limit_bytes=mib * MIB)


SCRATCH = [
    pltpu.VMEM((KEYS, 2 * HEAD), BF),
    pltpu.VMEM((HEAD, KEYS), BF),
    pltpu.VMEM((KEYS, HEAD), F32),
    pltpu.VMEM((KEYS, HEAD), F32),
    pltpu.VMEM((2, 8, HEAD), F32),
]


def shape(*dims, dtype=BF):
    return jax.ShapeDtypeStruct(dims, dtype)


def cost(us):
    return pl.CostEstimate(flops=0, bytes_accessed=int(us * 3_000_000), transcendentals=0)


def cost(us):
    return pl.CostEstimate(flops=0, bytes_accessed=int(us * 3_000_000), transcendentals=0)


def pack_a_call(*args):
    halo = shape(2, TILE, args[4].shape[1])
    return pl.pallas_call(
        pack_a_kernel,
        out_shape=(shape(ROWS_B, HEAD),) * SIDE + (halo, halo),
        in_specs=[SMEM] * 3 + [VMEM] + [ANY] * 5,
        out_specs=[ANY] * (SIDE + 2),
        scratch_shapes=[pltpu.VMEM((POS, WIDE), BF)] * 5
        + [
            pltpu.VMEM((SIDE, ROWS_B, HEAD), BF),
            pltpu.VMEM((2, *halo.shape), BF),
            pltpu.SemaphoreType.DMA((15,)),
        ],
        compiler_params=room(60),
        cost_estimate=cost(3),
        name="pack_a",
    )(*args)


def pack_b_call(*args):
    q = args[4]
    return pl.pallas_call(
        pack_b_kernel,
        out_shape=shape(GROUP, ROWS_B, HEAD),
        in_specs=[SMEM] * 3 + [VMEM] + [ANY] * 5,
        out_specs=ANY,
        scratch_shapes=[pltpu.VMEM(q.shape, BF)] * 5
        + [pltpu.VMEM((GROUP, ROWS_B, HEAD), BF), pltpu.SemaphoreType.DMA((24,))],
        compiler_params=room(60),
        cost_estimate=cost(4),
        name="pack_b",
    )(*args)


def four_call(kernel, rows, scratch, us, name, place, shares):
    return pl.pallas_call(
        kernel,
        out_shape=(rows,) * SIDE,
        in_specs=[SMEM] + [VMEM] * SIDE,
        out_specs=[VMEM] * SIDE,
        scratch_shapes=scratch,
        compiler_params=room(32),
        cost_estimate=cost(us),
        name=name,
    )(place, *shares)


def head_call(arrived):
    return pl.pallas_call(
        head_kernel,
        out_shape=shape(GROUP, BACK_B, HEAD),
        in_specs=[ANY],
        out_specs=ANY,
        scratch_shapes=[
            pltpu.VMEM((GROUP, ROWS_B, HEAD), BF),
            pltpu.VMEM((GROUP, BACK_B, HEAD), BF),
            pltpu.SemaphoreType.DMA((15,)),
        ]
        + SCRATCH,
        compiler_params=room(60),
        cost_estimate=cost(8),
        name="head",
    )(arrived)


def join_call(place, shares, b, sums, left, right):
    out = shape(*sums.shape[1:])
    return pl.pallas_call(
        join_kernel,
        out_shape=(out,) * 3,
        in_specs=[SMEM] + [ANY] * (SIDE + 4),
        out_specs=[ANY] * 3,
        scratch_shapes=[pltpu.VMEM((SIDE, BACK_B, HEAD), BF)]
        + [pltpu.VMEM(x.shape, x.dtype) for x in (b, sums, left, right)]
        + [pltpu.VMEM(sums.shape, BF), pltpu.SemaphoreType.DMA((38,))],
        compiler_params=room(60),
        cost_estimate=cost(4),
        name="join",
    )(place, *shares, b, sums, left, right)


def own_call(sides, q, k, v, o, g, before, after, lse):
    feature = q.shape[1]
    rows = pl.BlockSpec((POS, WIDE), lambda i: (0, i))
    edge = pl.BlockSpec((2, TILE, WIDE), lambda i: (0, 0, i))
    whole = pl.BlockSpec(lse.shape, lambda i: (0, 0, 0))
    halo = shape(2, TILE, feature)
    return pl.pallas_call(
        own_kernel,
        grid=(feature // WIDE,),
        out_shape=(shape(3, POS, feature, dtype=F32), halo, halo),
        in_specs=[SMEM] + [rows] * 5 + [edge, edge, whole],
        out_specs=[pl.BlockSpec((3, POS, WIDE), lambda i: (0, 0, i)), edge, edge],
        compiler_params=room(63),
        cost_estimate=cost(9),
        name="own",
    )(sides, q, k, v, o, g, before, after, lse)


def around(axis_step, shares):
    def partner(i, step):
        y, z = i // SIDE, i % SIDE
        return (y + step[0]) % SIDE * SIDE + (z + step[1]) % SIDE

    out = [shares[0], None, None, None]
    for d in (2, 1, 3):
        step = (d * axis_step[0], d * axis_step[1])
        out[d] = lax.ppermute(shares[d], "group", [(i, partner(i, step)) for i in range(GROUP)])
    return out


def body(query_rows, key_rows, value_rows, out_rows, grad_out, log_sum_exp, far_frames, far_blocks):
    rows = tuple(a[0] for a in (query_rows, key_rows, value_rows, out_rows, grad_out))
    lse = jnp.transpose(log_sum_exp, (1, 0, 2))
    inner = lax.axis_size("inner")
    inner_at = lax.axis_index("inner").astype(jnp.int32)
    group_at = lax.axis_index("group").astype(jnp.int32)
    sides = jnp.stack([inner_at, jnp.full((), inner, jnp.int32)])
    up = [(i, i + 1) for i in range(inner - 1)]
    down = [(i + 1, i) for i in range(inner - 1)]
    place = jnp.stack([group_at // SIDE, group_at % SIDE])
    facts = (place, far_frames[0], far_blocks[0], lse)

    *sends_z, first_rows, last_rows = pack_a_call(*facts, *rows)
    got_z = around((0, 1), sends_z)
    before = lax.ppermute(last_rows, "inner", up)
    after = lax.ppermute(first_rows, "inner", down)
    send_b = pack_b_call(*facts, *rows)
    send_b, got_z, before, after = lax.optimization_barrier((send_b, got_z, before, after))
    got_b = lax.all_to_all(send_b, "group", 0, 0, tiled=True)

    sends_y = four_call(split_kernel, shape(SIDE, ROWS_A, HEAD), [], 3, "split", place, got_z)
    got_y = around((1, 0), sends_y)
    sums, to_low, to_high = own_call(sides, *rows, before, after, lse)
    got_y, to_low, to_high = lax.optimization_barrier((got_y, to_low, to_high))
    from_right = lax.ppermute(to_low, "inner", down)
    from_left = lax.ppermute(to_high, "inner", up)
    scratch = [pltpu.VMEM((GROUP, HALF, HEAD), BF)] * 2 + SCRATCH
    back_y = four_call(quarter_kernel, shape(SIDE, ROWS_R, HEAD), scratch, 3, "quarter", place, got_y)
    home_y = around((-1, 0), back_y)
    scratch = [pltpu.VMEM((SIDE, 2, POS, HEAD), F32)]
    back_z = four_call(merge_kernel, shape(BACK_B, HEAD), scratch, 3, "merge", place, home_y)

    got_b, back_z = lax.optimization_barrier((got_b, back_z))
    home_z = around((0, -1), back_z)
    back_b, from_left, from_right = lax.optimization_barrier((head_call(got_b), from_left, from_right))
    home_b = lax.all_to_all(back_b, "group", 0, 0, tiled=True)
    return tuple(a[None] for a in join_call(place, home_z, home_b, sums, from_left, from_right))


def solution(mesh):
    shard = P("group", "inner", None)
    return jax.shard_map(
        body,
        mesh=mesh,
        in_specs=(shard,) * 5 + (P("group", None, "inner"), shard, shard),
        out_specs=(shard,) * 3,
        check_vma=False,
    )
```

```python
import functools
import math

import jax
import jax.numpy as jnp
from jax import lax
from jax.experimental import pallas as pl
from jax.experimental.pallas import tpu as pltpu
from jax.sharding import PartitionSpec as P

BF = jnp.bfloat16
F32 = jnp.float32
HEAD = 128
TILE = 64
HALF = 32
BLOCK = 8
GROUP = 16
SIDE = 4
POS = 128
WIDE = SIDE * HEAD
LOG2E = math.log2(math.e)
SCALE = 1.0 / math.sqrt(HEAD)
BIG = 1e30

BQ, BK, BV, BG, BS, ROWS_B = 0, 128, 256, 384, 512, 528
BACK_B = 384
AK, AV, AQ, AG, AS, ROWS_A = 0, 64, 128, 160, 192, 208
RK, RV, RQ, ROWS_R = 0, 64, 128, 160


def nt(a, b):
    return lax.dot_general(a, b, (((1,), (1,)), ((), ())), preferred_element_type=F32)


def nn(a, b):
    return jnp.dot(a, b, preferred_element_type=F32)


def cols(h):
    return pl.ds(h * HEAD, HEAD)


def three_terms(x):
    hi = x.astype(BF).astype(F32)
    mid = (x - hi).astype(BF).astype(F32)
    low = ((x - hi) - mid).astype(BF).astype(F32)
    return hi, mid, low


class Copies:
    def __init__(self, sems):
        self.sems, self.used, self.open = sems, 0, {}

    def start(self, key, source, target):
        copy = pltpu.make_async_copy(source, target, self.sems.at[self.used])
        copy.start()
        self.used += 1
        self.open.setdefault(key, []).append(copy)

    def wait(self, key):
        for copy in self.open.pop(key, []):
            copy.wait()

    def wait_all(self):
        for key in list(self.open):
            self.wait(key)


class Copies:
    def __init__(self, sems):
        self.sems, self.used, self.open = sems, 0, {}

    def start(self, key, source, target):
        copy = pltpu.make_async_copy(source, target, self.sems.at[self.used])
        copy.start()
        self.used += 1
        self.open.setdefault(key, []).append(copy)

    def wait(self, key):
        for copy in self.open.pop(key, []):
            copy.wait()

    def wait_all(self):
        for key in list(self.open):
            self.wait(key)


def deltas(grads, outs):
    ones = jnp.ones((8, HEAD), BF)
    prod = jnp.concatenate([g.astype(F32) * o.astype(F32) for g, o in zip(grads, outs)], 0)
    hi = prod.astype(BF)
    lo = (prod - hi.astype(F32)).astype(BF)
    sums = nt(ones, hi) + nt(ones, lo)
    return [sums[0:1, j * HEAD : j * HEAD + HEAD] for j in range(len(grads))]


def pair_masks(frame, frames_ref, blocks_ref):
    code = lax.broadcasted_iota(jnp.int32, (1, HEAD), 1)
    masks = []
    for t in range(POS // TILE):
        hit = jnp.abs(code // BLOCK - frame) == 1
        for j in range(frames_ref.shape[1]):
            hit = hit | (code == frames_ref[t, j] * BLOCK + blocks_ref[t, j])
        masks.append(hit.astype(F32))
    return masks


def stat_rows(lse, delta, masks):
    sub = lax.broadcasted_iota(jnp.int32, (16, HEAD), 0)
    rows = jnp.zeros((16, HEAD), F32)
    for i, term in enumerate(list(three_terms(lse) + three_terms(delta)) + masks):
        rows = jnp.where(sub == i, term, rows)
    return rows


def pack_a_kernel(
    group_ref, frames_ref, blocks_ref, lse_ref, q_hbm, k_hbm, v_hbm, o_hbm, g_hbm,
    z0_hbm, z1_hbm, z2_hbm, z3_hbm, low_hbm, high_hbm,
    q_all, k_all, v_all, o_all, g_all, send_ref, edge_ref, sems,
):
    copies = Copies(sems)
    at = slice(SIDE * WIDE, SIDE * WIDE + WIDE)
    for source, target in zip((g_hbm, o_hbm, q_hbm, k_hbm, v_hbm), (g_all, o_all, q_all, k_all, v_all)):
        copies.start("in", source.at[:, at], target)
    for i, source in enumerate((k_hbm, v_hbm)):
        copies.start("edge", source.at[0:TILE, :], edge_ref.at[0, i])
        copies.start("edge", source.at[POS - TILE : POS, :], edge_ref.at[1, i])
    masks = pair_masks(group_ref[0], frames_ref, blocks_ref)
    copies.wait("in")
    rows = deltas([g_all[:, cols(j)] for j in range(SIDE)], [o_all[:, cols(j)] for j in range(SIDE)])
    for j in range(SIDE):
        send_ref[j, BQ : BQ + POS, :] = q_all[:, cols(j)]
        send_ref[j, BK : BK + POS, :] = k_all[:, cols(j)]
        send_ref[j, BV : BV + POS, :] = v_all[:, cols(j)]
        send_ref[j, BG : BG + POS, :] = g_all[:, cols(j)]
        send_ref[j, BS:ROWS_B, :] = stat_rows(lse_ref[GROUP + j], rows[j], masks).astype(BF)
    for dz, out in enumerate((z0_hbm, z1_hbm, z2_hbm, z3_hbm)):
        copies.start("out", send_ref.at[lax.rem(group_ref[0] + dz, SIDE)], out)
    copies.wait("edge")
    copies.start("out", edge_ref.at[0], low_hbm)
    copies.start("out", edge_ref.at[1], high_hbm)
    copies.wait_all()


def pack_b_kernel(
    group_ref, frames_ref, blocks_ref, lse_ref, q_hbm, k_hbm, v_hbm, o_hbm, g_hbm, send_hbm,
    q_all, k_all, v_all, o_all, g_all, send_ref, sems,
):
    copies = Copies(sems)
    pairs = ((g_hbm, g_all), (o_hbm, o_all), (q_hbm, q_all), (k_hbm, k_all), (v_hbm, v_all))
    for block in range(SIDE):
        at = slice(block * WIDE, block * WIDE + WIDE)
        for source, target in pairs:
            copies.start(block, source.at[:, at], target.at[:, at])
    masks = pair_masks(group_ref[0], frames_ref, blocks_ref)
    for block in range(SIDE):
        copies.wait(block)
        heads = [block * SIDE + j for j in range(SIDE)]
        rows = deltas([g_all[:, cols(h)] for h in heads], [o_all[:, cols(h)] for h in heads])
        for j, h in enumerate(heads):
            send_ref[h, BQ : BQ + POS, :] = q_all[:, cols(h)]
            send_ref[h, BK : BK + POS, :] = k_all[:, cols(h)]
            send_ref[h, BV : BV + POS, :] = v_all[:, cols(h)]
            send_ref[h, BG : BG + POS, :] = g_all[:, cols(h)]
            send_ref[h, BS:ROWS_B, :] = stat_rows(lse_ref[h], rows[j], masks).astype(BF)
        four = slice(block * SIDE, block * SIDE + SIDE)
        copies.start("out", send_ref.at[four], send_hbm.at[four])
    copies.wait_all()


def split_kernel(group_ref, *refs):
    ins, outs = refs[:SIDE], refs[SIDE:]
    lane = lax.broadcasted_iota(jnp.int32, (16, HEAD), 1)
    sub = lax.broadcasted_iota(jnp.int32, (16, HEAD), 0)
    for dz, got in enumerate(ins):
        stats = got[BS:ROWS_B, :].astype(F32)
        for dy, out in enumerate(outs):
            y = lax.rem(group_ref[0] // SIDE + dy, SIDE)
            tile = pl.multiple_of((y // 2) * TILE, TILE)
            half = pl.multiple_of(y * HALF, HALF)
            out[dz, AK : AK + TILE, :] = got[pl.ds(BK + tile, TILE), :]
            out[dz, AV : AV + TILE, :] = got[pl.ds(BV + tile, TILE), :]
            out[dz, AQ : AQ + HALF, :] = got[pl.ds(BQ + half, HALF), :]
            out[dz, AG : AG + HALF, :] = got[pl.ds(BG + half, HALF), :]
            turned = pltpu.roll(stats, lax.rem(dz * HALF + HEAD - half, HEAD), 1)
            inside = (lane >= dz * HALF) & (lane < dz * HALF + HALF)
            kept = jnp.where(sub < 6, jnp.where(inside, turned, 0.0), stats)
            out[dz, AS:ROWS_A, :] = kept.astype(BF)


def own_kernel(
    side_ref, q_ref, k_ref, v_ref, o_ref, g_ref, before_ref, after_ref, lse_ref,
    sums_ref, low_ref, high_ref,
):
    step = pl.program_id(0)
    width = POS + 2 * TILE
    key = lax.broadcasted_iota(jnp.int32, (width, POS), 0)
    query = lax.broadcasted_iota(jnp.int32, (width, POS), 1)
    first = jnp.where(side_ref[0] > 0, 0, TILE)
    last = jnp.where(side_ref[0] < side_ref[1] - 1, width, width - TILE)
    inside = (key >= query) & (key <= query + 2 * TILE) & (key >= first) & (key < last)
    rows = deltas([g_ref[:, cols(j)] for j in range(SIDE)], [o_ref[:, cols(j)] for j in range(SIDE)])
    for j in range(SIDE):
        q = q_ref[:, cols(j)]
        g = g_ref[:, cols(j)]
        k = jnp.concatenate([before_ref[0, :, cols(j)], k_ref[:, cols(j)], after_ref[0, :, cols(j)]], 0)
        v = jnp.concatenate([before_ref[1, :, cols(j)], v_ref[:, cols(j)], after_ref[1, :, cols(j)]], 0)
        lse = lse_ref[step * SIDE + j]
        p = jnp.exp2(nt(k, q) * (SCALE * LOG2E) - lse * LOG2E)
        p = jnp.where(inside, p, 0.0)
        ds = (p * (nt(v, g) - rows[j])).astype(BF)
        dv = nn(p.astype(BF), g)
        dk = nn(ds, q) * SCALE
        dq = lax.dot_general(ds, k, (((0,), (0,)), ((), ())), preferred_element_type=F32)
        sums_ref[0, :, cols(j)] = dq * SCALE
        sums_ref[1, :, cols(j)] = dk[TILE : TILE + POS]
        sums_ref[2, :, cols(j)] = dv[TILE : TILE + POS]
        low_ref[0, :, cols(j)] = dk[0:TILE].astype(BF)
        low_ref[1, :, cols(j)] = dv[0:TILE].astype(BF)
        high_ref[0, :, cols(j)] = dk[TILE + POS :].astype(BF)
        high_ref[1, :, cols(j)] = dv[TILE + POS :].astype(BF)


CHUNK = 512
UNROLL = 2
KEYS = GROUP * TILE


def attend(span, queries, key_code, k, v, mask, rows, kx_ref, kt_ref, dk_ref, dv_ref, row_ref, put_dq):
    for s in range(2):
        row_ref[s] = rows[s]
    lane = lax.broadcasted_iota(jnp.int32, (KEYS, HEAD), 1)
    spread = (key_code == lane).astype(F32).astype(BF)
    padded = jnp.concatenate([mask.astype(F32), jnp.zeros((HEAD - GROUP, HEAD), F32)], 0)
    kx_ref[:, 0:HEAD] = k
    kx_ref[:, HEAD:] = ((nt(spread, padded.astype(BF)) - 1.0) * BIG).astype(BF)
    kt_ref[...] = k.astype(F32).T.astype(BF)
    dk_ref[...] = jnp.zeros_like(dk_ref)
    dv_ref[...] = jnp.zeros_like(dv_ref)
    count = CHUNK // span
    query = lax.broadcasted_iota(jnp.int32, (CHUNK, HEAD), 0) // span
    column = lax.broadcasted_iota(jnp.int32, (CHUNK, HEAD), 1)

    def one_chunk(c, carry):
        frames = pl.ds(c * count, count)
        q, g = queries(frames)
        choose = (column == query + c * count).astype(F32).astype(BF)
        qx = jnp.concatenate([q, choose], 1)
        lanes = CHUNK // HEAD
        lse, delta = (
            jnp.concatenate([row_ref[s, pl.ds(lanes * c + i, 1), :] for i in range(lanes)], 1) for s in range(2)
        )
        p = jnp.exp2(nt(kx_ref[...], qx) * (SCALE * LOG2E) - lse * LOG2E)
        ds = (p * (nt(v, g) - delta)).astype(BF)
        dv_ref[...] += nn(p.astype(BF), g)
        dk_ref[...] += nn(ds, q)
        put_dq(frames, (nn(kt_ref[...], ds) * SCALE).T.astype(BF).reshape(count, span, HEAD))
        return carry

    lax.fori_loop(0, GROUP * span // CHUNK, one_chunk, 0, unroll=UNROLL)


def added(stats, at):
    return (stats[:, at, :] + stats[:, at + 1, :]) + stats[:, at + 2, :]


def stacked(rows):
    rows = rows + [jnp.zeros((8 - len(rows), HEAD), F32)] if len(rows) < 8 else rows
    return jnp.concatenate(rows, 0)


def quarter_kernel(group_ref, *refs):
    ins, outs = refs[:SIDE], refs[SIDE : 2 * SIDE]
    q_ref, g_ref, kx_ref, kt_ref, dk_ref, dv_ref, row_ref = refs[2 * SIDE :]
    y, z = group_ref[0] // SIDE, lax.rem(group_ref[0], SIDE)
    stats = jnp.concatenate([got[:, AS:ROWS_A, :] for got in ins], 0).astype(F32)
    rows = []
    for s in range(2):
        full = added(stats, 3 * s)
        rows.append(
            stacked(
                [
                    (full[i : i + 1] + full[i + 1 : i + 2]) + (full[i + 2 : i + 3] + full[i + 3 : i + 4])
                    for i in range(0, GROUP, SIDE)
                ]
            )
        )
    mask = jnp.where(y >= 2, stats[:, 7, :], stats[:, 6, :])
    k = jnp.concatenate([got[:, AK : AK + TILE, :] for got in ins], 0)
    v = jnp.concatenate([got[:, AV : AV + TILE, :] for got in ins], 0)
    for i, got in enumerate(ins):
        q_ref[SIDE * i : SIDE * i + SIDE] = got[:, AQ : AQ + HALF, :]
        g_ref[SIDE * i : SIDE * i + SIDE] = got[:, AG : AG + HALF, :]
    row = lax.broadcasted_iota(jnp.int32, (KEYS, HEAD), 0)
    source_y = (y + SIDE - row // (SIDE * TILE)) % SIDE
    source_z = (z + SIDE - (row // TILE) % SIDE) % SIDE
    key_code = (source_y * SIDE + source_z) * BLOCK + (row % TILE) // BLOCK

    def queries(frames):
        return q_ref[frames].reshape(CHUNK, HEAD), g_ref[frames].reshape(CHUNK, HEAD)

    def put_dq(frames, dq):
        q_ref[frames] = dq

    attend(
        HALF, queries, key_code, k.reshape(KEYS, HEAD), v.reshape(KEYS, HEAD), mask, rows,
        kx_ref, kt_ref, dk_ref, dv_ref, row_ref, put_dq,
    )
    span = SIDE * TILE
    for i, out in enumerate(outs):
        dk = (dk_ref[i * span : i * span + span] * SCALE).astype(BF)
        dv = dv_ref[i * span : i * span + span].astype(BF)
        out[:, RK : RK + TILE, :] = dk.reshape(SIDE, TILE, HEAD)
        out[:, RV : RV + TILE, :] = dv.reshape(SIDE, TILE, HEAD)
        out[:, RQ : RQ + HALF, :] = q_ref[SIDE * i : SIDE * i + SIDE]


def merge_kernel(group_ref, *refs):
    ins, outs, sum_ref = refs[:SIDE], refs[SIDE : 2 * SIDE], refs[2 * SIDE]
    sum_ref[...] = jnp.zeros_like(sum_ref)
    for dy, got in enumerate(ins):
        y = lax.rem(group_ref[0] // SIDE + dy, SIDE)
        tile = pl.multiple_of((y // 2) * TILE, TILE)
        half = pl.multiple_of(y * HALF, HALF)
        for dz, out in enumerate(outs):
            out[pl.ds(BQ + half, HALF), :] = got[dz, RQ:ROWS_R, :]
            sum_ref[dz, 0, pl.ds(tile, TILE), :] += got[dz, RK : RK + TILE, :].astype(F32)
            sum_ref[dz, 1, pl.ds(tile, TILE), :] += got[dz, RV : RV + TILE, :].astype(F32)
    for dz, out in enumerate(outs):
        out[BK : BK + POS, :] = sum_ref[dz, 0].astype(BF)
        out[BV : BV + POS, :] = sum_ref[dz, 1].astype(BF)


def head_kernel(in_hbm, out_hbm, in_ref, out_ref, sems, *scratch):
    copies = Copies(sems)

    def fetch(key, first, count):
        copies.start(key, in_hbm.at[:, first : first + count, :], in_ref.at[:, first : first + count, :])

    fetch("stats", BS, ROWS_B - BS)
    for unit in range(2):
        for at in (BK, BV, BQ, BG):
            fetch(unit, at + unit * TILE, TILE)
    key_code = lax.broadcasted_iota(jnp.int32, (KEYS, HEAD), 0) // BLOCK
    lane = lax.broadcasted_iota(jnp.int32, (1, HEAD), 1)
    copies.wait("stats")
    stats = in_ref[:, BS:ROWS_B, :].astype(F32)
    for unit in range(2):
        at = unit * TILE
        rows = []
        for s in range(2):
            full = added(stats, 3 * s)
            turned = pltpu.roll(full, TILE, 1)
            left, right = (full, turned) if unit == 0 else (turned, full)
            rows.append(
                stacked(
                    [jnp.where(lane < TILE, left[i : i + 1], right[i + 1 : i + 2]) for i in range(0, GROUP, 2)]
                )
            )

        def queries(frames):
            q = in_ref[frames, BQ + at : BQ + at + TILE, :].reshape(CHUNK, HEAD)
            g = in_ref[frames, BG + at : BG + at + TILE, :].reshape(CHUNK, HEAD)
            return q, g

        def put_dq(frames, dq):
            out_ref[frames, BQ + at : BQ + at + TILE, :] = dq

        copies.wait(unit)
        attend(
            TILE, queries, key_code,
            in_ref[:, BK + at : BK + at + TILE, :].reshape(KEYS, HEAD),
            in_ref[:, BV + at : BV + at + TILE, :].reshape(KEYS, HEAD),
            stats[:, 6 + unit, :], rows, *scratch, put_dq,
        )
        dk_ref, dv_ref = scratch[2:4]
        dk = (dk_ref[...] * SCALE).astype(BF).reshape(GROUP, TILE, HEAD)
        out_ref[:, BK + at : BK + at + TILE, :] = dk
        out_ref[:, BV + at : BV + at + TILE, :] = dv_ref[...].astype(BF).reshape(GROUP, TILE, HEAD)
        for first in (BQ + at, BK + at, BV + at):
            part = slice(first, first + TILE)
            copies.start("out", out_ref.at[:, part, :], out_hbm.at[:, part, :])
    copies.wait_all()


def settle_kernel(sums_ref, left_ref, right_ref, out_ref):
    out_ref[0] = sums_ref[0].astype(BF)
    for i in range(2):
        edges = jnp.concatenate([left_ref[i], right_ref[i]], 0).astype(F32)
        out_ref[1 + i] = (sums_ref[1 + i] + edges).astype(BF)


def join_kernel(
    group_ref, z0_hbm, z1_hbm, z2_hbm, z3_hbm, b_hbm, base_in, dq_out, dk_out, dv_out,
    a_ref, b_ref, base_ref, low_ref, sems,
):
    copies = Copies(sems)
    z = lax.rem(group_ref[0], SIDE)
    sets = ((dq_out, BQ), (dk_out, BK), (dv_out, BV))
    order = [SIDE] + list(range(SIDE))
    for block in order:
        at = slice(block * WIDE, block * WIDE + WIDE)
        if block == SIDE:
            for dz, share in enumerate((z0_hbm, z1_hbm, z2_hbm, z3_hbm)):
                copies.start(block, share, a_ref.at[dz])
        else:
            four = slice(SIDE * block, SIDE * block + SIDE)
            copies.start(block, b_hbm.at[four], b_ref.at[four])
        copies.start(block, base_in.at[:, :, at], base_ref.at[:, :, at])
    for block in order:
        copies.wait(block)
        at = slice(block * WIDE, block * WIDE + WIDE)
        for which, (out, row) in enumerate(sets):
            for j in range(SIDE):
                h = SIDE * block + j
                if block < SIDE:
                    more = b_ref[h, row : row + POS, :]
                else:
                    more = a_ref[lax.rem(j + SIDE - z, SIDE), row : row + POS, :]
                total = base_ref[which, :, cols(h)].astype(F32) + more.astype(F32)
                low_ref[which, :, cols(h)] = total.astype(BF)
            copies.start("out", low_ref.at[which, :, at], out.at[:, at])
    copies.wait_all()


VMEM = pl.BlockSpec(memory_space=pltpu.VMEM)
SMEM = pl.BlockSpec(memory_space=pltpu.SMEM)
ANY = pl.BlockSpec(memory_space=pl.ANY)
MIB = 1024 * 1024


def room(mib):
    return pltpu.CompilerParams(vmem_limit_bytes=mib * MIB)


SCRATCH = [
    pltpu.VMEM((KEYS, 2 * HEAD), BF),
    pltpu.VMEM((HEAD, KEYS), BF),
    pltpu.VMEM((KEYS, HEAD), F32),
    pltpu.VMEM((KEYS, HEAD), F32),
    pltpu.VMEM((2, 8, HEAD), F32),
]


def shape(*dims, dtype=BF):
    return jax.ShapeDtypeStruct(dims, dtype)


def cost(us):
    return pl.CostEstimate(flops=0, bytes_accessed=int(us * 3_000_000), transcendentals=0)


def cost(us):
    return pl.CostEstimate(flops=0, bytes_accessed=int(us * 3_000_000), transcendentals=0)


def pack_a_call(*args):
    halo = shape(2, TILE, args[4].shape[1])
    return pl.pallas_call(
        pack_a_kernel,
        out_shape=(shape(ROWS_B, HEAD),) * SIDE + (halo, halo),
        in_specs=[SMEM] * 3 + [VMEM] + [ANY] * 5,
        out_specs=[ANY] * (SIDE + 2),
        scratch_shapes=[pltpu.VMEM((POS, WIDE), BF)] * 5
        + [
            pltpu.VMEM((SIDE, ROWS_B, HEAD), BF),
            pltpu.VMEM((2, *halo.shape), BF),
            pltpu.SemaphoreType.DMA((15,)),
        ],
        compiler_params=room(60),
        cost_estimate=cost(3),
        name="pack_a",
    )(*args)


def pack_b_call(*args):
    q = args[4]
    return pl.pallas_call(
        pack_b_kernel,
        out_shape=shape(GROUP, ROWS_B, HEAD),
        in_specs=[SMEM] * 3 + [VMEM] + [ANY] * 5,
        out_specs=ANY,
        scratch_shapes=[pltpu.VMEM(q.shape, BF)] * 5
        + [pltpu.VMEM((GROUP, ROWS_B, HEAD), BF), pltpu.SemaphoreType.DMA((24,))],
        compiler_params=room(60),
        cost_estimate=cost(4),
        name="pack_b",
    )(*args)


def four_call(kernel, rows, scratch, us, name, place, shares):
    return pl.pallas_call(
        kernel,
        out_shape=(rows,) * SIDE,
        in_specs=[SMEM] + [VMEM] * SIDE,
        out_specs=[VMEM] * SIDE,
        scratch_shapes=scratch,
        compiler_params=room(32),
        cost_estimate=cost(us),
        name=name,
    )(place, *shares)


def head_call(arrived):
    return pl.pallas_call(
        head_kernel,
        out_shape=shape(GROUP, BACK_B, HEAD),
        in_specs=[ANY],
        out_specs=ANY,
        scratch_shapes=[
            pltpu.VMEM((GROUP, ROWS_B, HEAD), BF),
            pltpu.VMEM((GROUP, BACK_B, HEAD), BF),
            pltpu.SemaphoreType.DMA((15,)),
        ]
        + SCRATCH,
        compiler_params=room(60),
        cost_estimate=cost(8),
        name="head",
    )(arrived)


def settle_call(sums, left, right):
    edge = pl.BlockSpec((2, TILE, WIDE), lambda i: (0, 0, i))
    rows = pl.BlockSpec((3, POS, WIDE), lambda i: (0, 0, i))
    return pl.pallas_call(
        settle_kernel,
        grid=(sums.shape[2] // WIDE,),
        out_shape=shape(*sums.shape),
        in_specs=[rows, edge, edge],
        out_specs=rows,
        compiler_params=room(60),
        cost_estimate=cost(4),
        name="settle",
    )(sums, left, right)


def join_call(group, shares, b, base):
    out = shape(*base.shape[1:])
    return pl.pallas_call(
        join_kernel,
        out_shape=(out,) * 3,
        in_specs=[SMEM] + [ANY] * (SIDE + 2),
        out_specs=[ANY] * 3,
        scratch_shapes=[pltpu.VMEM((SIDE, BACK_B, HEAD), BF)]
        + [pltpu.VMEM(x.shape, x.dtype) for x in (b, base, base)]
        + [pltpu.SemaphoreType.DMA((28,))],
        compiler_params=room(60),
        cost_estimate=cost(4),
        name="join",
    )(group, *shares, b, base)


def own_call(sides, q, k, v, o, g, before, after, lse):
    feature = q.shape[1]
    rows = pl.BlockSpec((POS, WIDE), lambda i: (0, i))
    edge = pl.BlockSpec((2, TILE, WIDE), lambda i: (0, 0, i))
    whole = pl.BlockSpec(lse.shape, lambda i: (0, 0, 0))
    halo = shape(2, TILE, feature)
    return pl.pallas_call(
        own_kernel,
        grid=(feature // WIDE,),
        out_shape=(shape(3, POS, feature, dtype=F32), halo, halo),
        in_specs=[SMEM] + [rows] * 5 + [edge, edge, whole],
        out_specs=[pl.BlockSpec((3, POS, WIDE), lambda i: (0, 0, i)), edge, edge],
        compiler_params=room(63),
        cost_estimate=cost(9),
        name="own",
    )(sides, q, k, v, o, g, before, after, lse)


def around(axis_step, shares):
    def partner(i, step):
        y, z = i // SIDE, i % SIDE
        return (y + step[0]) % SIDE * SIDE + (z + step[1]) % SIDE

    out = [shares[0], None, None, None]
    for d in (2, 1, 3):
        step = (d * axis_step[0], d * axis_step[1])
        out[d] = lax.ppermute(shares[d], "group", [(i, partner(i, step)) for i in range(GROUP)])
    return out


def body(query_rows, key_rows, value_rows, out_rows, grad_out, log_sum_exp, far_frames, far_blocks):
    rows = tuple(a[0] for a in (query_rows, key_rows, value_rows, out_rows, grad_out))
    lse = jnp.transpose(log_sum_exp, (1, 0, 2))
    inner = lax.axis_size("inner")
    inner_at = lax.axis_index("inner").astype(jnp.int32)
    group_at = lax.axis_index("group").astype(jnp.int32)
    sides = jnp.stack([inner_at, jnp.full((), inner, jnp.int32)])
    up = [(i, i + 1) for i in range(inner - 1)]
    down = [(i + 1, i) for i in range(inner - 1)]
    group = group_at.reshape(1)
    facts = (group, far_frames[0], far_blocks[0], lse)

    *sends_z, first_rows, last_rows = pack_a_call(*facts, *rows)
    got_z = around((0, 1), sends_z)
    before = lax.ppermute(last_rows, "inner", up)
    after = lax.ppermute(first_rows, "inner", down)
    send_b = pack_b_call(*facts, *rows)
    send_b, got_z, before, after = lax.optimization_barrier((send_b, got_z, before, after))
    got_b = lax.all_to_all(send_b, "group", 0, 0, tiled=True)

    sends_y = four_call(split_kernel, shape(SIDE, ROWS_A, HEAD), [], 3, "split", group, got_z)
    got_y = around((1, 0), sends_y)
    sums, to_low, to_high = own_call(sides, *rows, before, after, lse)
    got_y, to_low, to_high = lax.optimization_barrier((got_y, to_low, to_high))
    scratch = [pltpu.VMEM((GROUP, HALF, HEAD), BF)] * 2 + SCRATCH
    back_y = four_call(quarter_kernel, shape(SIDE, ROWS_R, HEAD), scratch, 3, "quarter", group, got_y)
    back_y, to_low, to_high = lax.optimization_barrier((back_y, to_low, to_high))
    home_y = around((-1, 0), back_y)
    from_right = lax.ppermute(to_low, "inner", down)
    from_left = lax.ppermute(to_high, "inner", up)
    scratch = [pltpu.VMEM((SIDE, 2, POS, HEAD), F32)]
    back_z = four_call(merge_kernel, shape(BACK_B, HEAD), scratch, 3, "merge", group, home_y)

    got_b, back_z = lax.optimization_barrier((got_b, back_z))
    home_z = around((0, -1), back_z)
    back_b, from_left, from_right = lax.optimization_barrier((head_call(got_b), from_left, from_right))
    home_b = lax.all_to_all(back_b, "group", 0, 0, tiled=True)
    base = settle_call(sums, from_left, from_right)
    return tuple(a[None] for a in join_call(group, home_z, home_b, base))


def solution(mesh):
    shard = P("group", "inner", None)
    return jax.shard_map(
        body,
        mesh=mesh,
        in_specs=(shard,) * 5 + (P("group", None, "inner"), shard, shard),
        out_specs=(shard,) * 3,
        check_vma=False,
    )
```

```python
import functools
import math

import jax
import jax.numpy as jnp
from jax import lax
from jax.experimental import pallas as pl
from jax.experimental.pallas import tpu as pltpu
from jax.sharding import PartitionSpec as P

BF = jnp.bfloat16
F32 = jnp.float32
HEAD = 128
TILE = 64
HALF = 32
BLOCK = 8
GROUP = 16
SIDE = 4
POS = 128
WIDE = SIDE * HEAD
LOG2E = math.log2(math.e)
SCALE = 1.0 / math.sqrt(HEAD)
BIG = 1e30

BQ, BK, BV, BG, BS, ROWS_B = 0, 128, 256, 384, 512, 528
BACK_B = 384
AK, AV, AQ, AG, AS, ROWS_A = 0, 64, 128, 160, 192, 208
RK, RV, RQ, ROWS_R = 0, 64, 128, 160


def nt(a, b):
    return lax.dot_general(a, b, (((1,), (1,)), ((), ())), preferred_element_type=F32)


def nn(a, b):
    return jnp.dot(a, b, preferred_element_type=F32)


def cols(h):
    return pl.ds(h * HEAD, HEAD)


def three_terms(x):
    hi = x.astype(BF).astype(F32)
    mid = (x - hi).astype(BF).astype(F32)
    low = ((x - hi) - mid).astype(BF).astype(F32)
    return hi, mid, low


class Copies:
    def __init__(self, sems):
        self.sems, self.used, self.open = sems, 0, {}

    def start(self, key, source, target):
        copy = pltpu.make_async_copy(source, target, self.sems.at[self.used])
        copy.start()
        self.used += 1
        self.open.setdefault(key, []).append(copy)

    def wait(self, key):
        for copy in self.open.pop(key, []):
            copy.wait()

    def wait_all(self):
        for key in list(self.open):
            self.wait(key)


class Copies:
    def __init__(self, sems):
        self.sems, self.used, self.open = sems, 0, {}

    def start(self, key, source, target):
        copy = pltpu.make_async_copy(source, target, self.sems.at[self.used])
        copy.start()
        self.used += 1
        self.open.setdefault(key, []).append(copy)

    def wait(self, key):
        for copy in self.open.pop(key, []):
            copy.wait()

    def wait_all(self):
        for key in list(self.open):
            self.wait(key)


def deltas(grads, outs):
    ones = jnp.ones((8, HEAD), BF)
    prod = jnp.concatenate([g.astype(F32) * o.astype(F32) for g, o in zip(grads, outs)], 0)
    hi = prod.astype(BF)
    lo = (prod - hi.astype(F32)).astype(BF)
    sums = nt(ones, hi) + nt(ones, lo)
    return [sums[0:1, j * HEAD : j * HEAD + HEAD] for j in range(len(grads))]


def pair_masks(frame, frames_ref, blocks_ref):
    code = lax.broadcasted_iota(jnp.int32, (1, HEAD), 1)
    masks = []
    for t in range(POS // TILE):
        hit = jnp.abs(code // BLOCK - frame) == 1
        for j in range(frames_ref.shape[1]):
            hit = hit | (code == frames_ref[t, j] * BLOCK + blocks_ref[t, j])
        masks.append(hit.astype(F32))
    return masks


def stat_rows(lse, delta, masks):
    sub = lax.broadcasted_iota(jnp.int32, (16, HEAD), 0)
    rows = jnp.zeros((16, HEAD), F32)
    for i, term in enumerate(list(three_terms(lse) + three_terms(delta)) + masks):
        rows = jnp.where(sub == i, term, rows)
    return rows


def pack_a_kernel(
    group_ref, frames_ref, blocks_ref, lse_ref, q_hbm, k_hbm, v_hbm, o_hbm, g_hbm,
    z0_hbm, z1_hbm, z2_hbm, z3_hbm, low_hbm, high_hbm,
    q_all, k_all, v_all, o_all, g_all, send_ref, edge_ref, sems,
):
    copies = Copies(sems)
    at = slice(SIDE * WIDE, SIDE * WIDE + WIDE)
    for source, target in zip((g_hbm, o_hbm, q_hbm, k_hbm, v_hbm), (g_all, o_all, q_all, k_all, v_all)):
        copies.start("in", source.at[:, at], target)
    for i, source in enumerate((k_hbm, v_hbm)):
        copies.start("edge", source.at[0:TILE, :], edge_ref.at[0, i])
        copies.start("edge", source.at[POS - TILE : POS, :], edge_ref.at[1, i])
    masks = pair_masks(group_ref[0], frames_ref, blocks_ref)
    copies.wait("in")
    rows = deltas([g_all[:, cols(j)] for j in range(SIDE)], [o_all[:, cols(j)] for j in range(SIDE)])
    for j in range(SIDE):
        send_ref[j, BQ : BQ + POS, :] = q_all[:, cols(j)]
        send_ref[j, BK : BK + POS, :] = k_all[:, cols(j)]
        send_ref[j, BV : BV + POS, :] = v_all[:, cols(j)]
        send_ref[j, BG : BG + POS, :] = g_all[:, cols(j)]
        send_ref[j, BS:ROWS_B, :] = stat_rows(lse_ref[GROUP + j], rows[j], masks).astype(BF)
    for dz, out in enumerate((z0_hbm, z1_hbm, z2_hbm, z3_hbm)):
        copies.start("out", send_ref.at[lax.rem(group_ref[0] + dz, SIDE)], out)
    copies.wait("edge")
    copies.start("out", edge_ref.at[0], low_hbm)
    copies.start("out", edge_ref.at[1], high_hbm)
    copies.wait_all()


def pack_b_kernel(
    group_ref, frames_ref, blocks_ref, lse_ref, q_hbm, k_hbm, v_hbm, o_hbm, g_hbm, send_hbm,
    q_all, k_all, v_all, o_all, g_all, send_ref, sems,
):
    copies = Copies(sems)
    pairs = ((g_hbm, g_all), (o_hbm, o_all), (q_hbm, q_all), (k_hbm, k_all), (v_hbm, v_all))
    for block in range(SIDE):
        at = slice(block * WIDE, block * WIDE + WIDE)
        for source, target in pairs:
            copies.start(block, source.at[:, at], target.at[:, at])
    masks = pair_masks(group_ref[0], frames_ref, blocks_ref)
    for block in range(SIDE):
        copies.wait(block)
        heads = [block * SIDE + j for j in range(SIDE)]
        rows = deltas([g_all[:, cols(h)] for h in heads], [o_all[:, cols(h)] for h in heads])
        for j, h in enumerate(heads):
            send_ref[h, BQ : BQ + POS, :] = q_all[:, cols(h)]
            send_ref[h, BK : BK + POS, :] = k_all[:, cols(h)]
            send_ref[h, BV : BV + POS, :] = v_all[:, cols(h)]
            send_ref[h, BG : BG + POS, :] = g_all[:, cols(h)]
            send_ref[h, BS:ROWS_B, :] = stat_rows(lse_ref[h], rows[j], masks).astype(BF)
        four = slice(block * SIDE, block * SIDE + SIDE)
        copies.start("out", send_ref.at[four], send_hbm.at[four])
    copies.wait_all()


def split_kernel(group_ref, *refs):
    ins, outs = refs[:SIDE], refs[SIDE:]
    lane = lax.broadcasted_iota(jnp.int32, (16, HEAD), 1)
    sub = lax.broadcasted_iota(jnp.int32, (16, HEAD), 0)
    for dz, got in enumerate(ins):
        stats = got[BS:ROWS_B, :].astype(F32)
        for dy, out in enumerate(outs):
            y = lax.rem(group_ref[0] // SIDE + dy, SIDE)
            tile = pl.multiple_of((y // 2) * TILE, TILE)
            half = pl.multiple_of(y * HALF, HALF)
            out[dz, AK : AK + TILE, :] = got[pl.ds(BK + tile, TILE), :]
            out[dz, AV : AV + TILE, :] = got[pl.ds(BV + tile, TILE), :]
            out[dz, AQ : AQ + HALF, :] = got[pl.ds(BQ + half, HALF), :]
            out[dz, AG : AG + HALF, :] = got[pl.ds(BG + half, HALF), :]
            turned = pltpu.roll(stats, lax.rem(dz * HALF + HEAD - half, HEAD), 1)
            inside = (lane >= dz * HALF) & (lane < dz * HALF + HALF)
            kept = jnp.where(sub < 6, jnp.where(inside, turned, 0.0), stats)
            out[dz, AS:ROWS_A, :] = kept.astype(BF)


def own_kernel(
    inner, at_ref, q_ref, k_ref, v_ref, o_ref, g_ref, before_ref, after_ref, lse_ref,
    sums_ref, low_ref, high_ref,
):
    step = pl.program_id(0)
    width = POS + 2 * TILE
    key = lax.broadcasted_iota(jnp.int32, (width, POS), 0)
    query = lax.broadcasted_iota(jnp.int32, (width, POS), 1)
    first = jnp.where(at_ref[0] > 0, 0, TILE)
    last = jnp.where(at_ref[0] < inner - 1, width, width - TILE)
    inside = (key >= query) & (key <= query + 2 * TILE) & (key >= first) & (key < last)
    rows = deltas([g_ref[:, cols(j)] for j in range(SIDE)], [o_ref[:, cols(j)] for j in range(SIDE)])
    for j in range(SIDE):
        q = q_ref[:, cols(j)]
        g = g_ref[:, cols(j)]
        k = jnp.concatenate([before_ref[0, :, cols(j)], k_ref[:, cols(j)], after_ref[0, :, cols(j)]], 0)
        v = jnp.concatenate([before_ref[1, :, cols(j)], v_ref[:, cols(j)], after_ref[1, :, cols(j)]], 0)
        lse = lse_ref[step * SIDE + j]
        p = jnp.exp2(nt(k, q) * (SCALE * LOG2E) - lse * LOG2E)
        p = jnp.where(inside, p, 0.0)
        ds = (p * (nt(v, g) - rows[j])).astype(BF)
        dv = nn(p.astype(BF), g)
        dk = nn(ds, q) * SCALE
        dq = lax.dot_general(ds, k, (((0,), (0,)), ((), ())), preferred_element_type=F32)
        sums_ref[0, :, cols(j)] = dq * SCALE
        sums_ref[1, :, cols(j)] = dk[TILE : TILE + POS]
        sums_ref[2, :, cols(j)] = dv[TILE : TILE + POS]
        low_ref[0, :, cols(j)] = dk[0:TILE].astype(BF)
        low_ref[1, :, cols(j)] = dv[0:TILE].astype(BF)
        high_ref[0, :, cols(j)] = dk[TILE + POS :].astype(BF)
        high_ref[1, :, cols(j)] = dv[TILE + POS :].astype(BF)


CHUNK = 512
UNROLL = 2
KEYS = GROUP * TILE


def attend(span, queries, key_code, k, v, mask, rows, kx_ref, kt_ref, dk_ref, dv_ref, row_ref, put_dq):
    for s in range(2):
        row_ref[s] = rows[s]
    lane = lax.broadcasted_iota(jnp.int32, (KEYS, HEAD), 1)
    spread = (key_code == lane).astype(F32).astype(BF)
    padded = jnp.concatenate([mask.astype(F32), jnp.zeros((HEAD - GROUP, HEAD), F32)], 0)
    kx_ref[:, 0:HEAD] = k
    kx_ref[:, HEAD:] = ((nt(spread, padded.astype(BF)) - 1.0) * BIG).astype(BF)
    kt_ref[...] = k.astype(F32).T.astype(BF)
    dk_ref[...] = jnp.zeros_like(dk_ref)
    dv_ref[...] = jnp.zeros_like(dv_ref)
    count = CHUNK // span
    query = lax.broadcasted_iota(jnp.int32, (CHUNK, HEAD), 0) // span
    column = lax.broadcasted_iota(jnp.int32, (CHUNK, HEAD), 1)

    def one_chunk(c, carry):
        frames = pl.ds(c * count, count)
        q, g = queries(frames)
        choose = (column == query + c * count).astype(F32).astype(BF)
        qx = jnp.concatenate([q, choose], 1)
        lanes = CHUNK // HEAD
        lse, delta = (
            jnp.concatenate([row_ref[s, pl.ds(lanes * c + i, 1), :] for i in range(lanes)], 1) for s in range(2)
        )
        p = jnp.exp2(nt(kx_ref[...], qx) * (SCALE * LOG2E) - lse * LOG2E)
        ds = (p * (nt(v, g) - delta)).astype(BF)
        dv_ref[...] += nn(p.astype(BF), g)
        dk_ref[...] += nn(ds, q)
        put_dq(frames, (nn(kt_ref[...], ds) * SCALE).T.astype(BF).reshape(count, span, HEAD))
        return carry

    lax.fori_loop(0, GROUP * span // CHUNK, one_chunk, 0, unroll=UNROLL)


def added(stats, at):
    return (stats[:, at, :] + stats[:, at + 1, :]) + stats[:, at + 2, :]


def stacked(rows):
    rows = rows + [jnp.zeros((8 - len(rows), HEAD), F32)] if len(rows) < 8 else rows
    return jnp.concatenate(rows, 0)


def quarter_kernel(group_ref, *refs):
    ins, outs = refs[:SIDE], refs[SIDE : 2 * SIDE]
    q_ref, g_ref, kx_ref, kt_ref, dk_ref, dv_ref, row_ref = refs[2 * SIDE :]
    y, z = group_ref[0] // SIDE, lax.rem(group_ref[0], SIDE)
    stats = jnp.concatenate([got[:, AS:ROWS_A, :] for got in ins], 0).astype(F32)
    rows = []
    for s in range(2):
        full = added(stats, 3 * s)
        rows.append(
            stacked(
                [
                    (full[i : i + 1] + full[i + 1 : i + 2]) + (full[i + 2 : i + 3] + full[i + 3 : i + 4])
                    for i in range(0, GROUP, SIDE)
                ]
            )
        )
    mask = jnp.where(y >= 2, stats[:, 7, :], stats[:, 6, :])
    k = jnp.concatenate([got[:, AK : AK + TILE, :] for got in ins], 0)
    v = jnp.concatenate([got[:, AV : AV + TILE, :] for got in ins], 0)
    for i, got in enumerate(ins):
        q_ref[SIDE * i : SIDE * i + SIDE] = got[:, AQ : AQ + HALF, :]
        g_ref[SIDE * i : SIDE * i + SIDE] = got[:, AG : AG + HALF, :]
    row = lax.broadcasted_iota(jnp.int32, (KEYS, HEAD), 0)
    source_y = (y + SIDE - row // (SIDE * TILE)) % SIDE
    source_z = (z + SIDE - (row // TILE) % SIDE) % SIDE
    key_code = (source_y * SIDE + source_z) * BLOCK + (row % TILE) // BLOCK

    def queries(frames):
        return q_ref[frames].reshape(CHUNK, HEAD), g_ref[frames].reshape(CHUNK, HEAD)

    def put_dq(frames, dq):
        q_ref[frames] = dq

    attend(
        HALF, queries, key_code, k.reshape(KEYS, HEAD), v.reshape(KEYS, HEAD), mask, rows,
        kx_ref, kt_ref, dk_ref, dv_ref, row_ref, put_dq,
    )
    span = SIDE * TILE
    for i, out in enumerate(outs):
        dk = (dk_ref[i * span : i * span + span] * SCALE).astype(BF)
        dv = dv_ref[i * span : i * span + span].astype(BF)
        out[:, RK : RK + TILE, :] = dk.reshape(SIDE, TILE, HEAD)
        out[:, RV : RV + TILE, :] = dv.reshape(SIDE, TILE, HEAD)
        out[:, RQ : RQ + HALF, :] = q_ref[SIDE * i : SIDE * i + SIDE]


def merge_kernel(group_ref, *refs):
    ins, outs, sum_ref = refs[:SIDE], refs[SIDE : 2 * SIDE], refs[2 * SIDE]
    sum_ref[...] = jnp.zeros_like(sum_ref)
    for dy, got in enumerate(ins):
        y = lax.rem(group_ref[0] // SIDE + dy, SIDE)
        tile = pl.multiple_of((y // 2) * TILE, TILE)
        half = pl.multiple_of(y * HALF, HALF)
        for dz, out in enumerate(outs):
            out[pl.ds(BQ + half, HALF), :] = got[dz, RQ:ROWS_R, :]
            sum_ref[dz, 0, pl.ds(tile, TILE), :] += got[dz, RK : RK + TILE, :].astype(F32)
            sum_ref[dz, 1, pl.ds(tile, TILE), :] += got[dz, RV : RV + TILE, :].astype(F32)
    for dz, out in enumerate(outs):
        out[BK : BK + POS, :] = sum_ref[dz, 0].astype(BF)
        out[BV : BV + POS, :] = sum_ref[dz, 1].astype(BF)


def head_kernel(in_hbm, out_hbm, in_ref, out_ref, sems, *scratch):
    copies = Copies(sems)

    def fetch(key, first, count):
        copies.start(key, in_hbm.at[:, first : first + count, :], in_ref.at[:, first : first + count, :])

    fetch("stats", BS, ROWS_B - BS)
    for unit in range(2):
        for at in (BK, BV, BQ, BG):
            fetch(unit, at + unit * TILE, TILE)
    key_code = lax.broadcasted_iota(jnp.int32, (KEYS, HEAD), 0) // BLOCK
    lane = lax.broadcasted_iota(jnp.int32, (1, HEAD), 1)
    copies.wait("stats")
    stats = in_ref[:, BS:ROWS_B, :].astype(F32)
    for unit in range(2):
        at = unit * TILE
        rows = []
        for s in range(2):
            full = added(stats, 3 * s)
            turned = pltpu.roll(full, TILE, 1)
            left, right = (full, turned) if unit == 0 else (turned, full)
            rows.append(
                stacked(
                    [jnp.where(lane < TILE, left[i : i + 1], right[i + 1 : i + 2]) for i in range(0, GROUP, 2)]
                )
            )

        def queries(frames):
            q = in_ref[frames, BQ + at : BQ + at + TILE, :].reshape(CHUNK, HEAD)
            g = in_ref[frames, BG + at : BG + at + TILE, :].reshape(CHUNK, HEAD)
            return q, g

        def put_dq(frames, dq):
            out_ref[frames, BQ + at : BQ + at + TILE, :] = dq

        copies.wait(unit)
        attend(
            TILE, queries, key_code,
            in_ref[:, BK + at : BK + at + TILE, :].reshape(KEYS, HEAD),
            in_ref[:, BV + at : BV + at + TILE, :].reshape(KEYS, HEAD),
            stats[:, 6 + unit, :], rows, *scratch, put_dq,
        )
        dk_ref, dv_ref = scratch[2:4]
        dk = (dk_ref[...] * SCALE).astype(BF).reshape(GROUP, TILE, HEAD)
        out_ref[:, BK + at : BK + at + TILE, :] = dk
        out_ref[:, BV + at : BV + at + TILE, :] = dv_ref[...].astype(BF).reshape(GROUP, TILE, HEAD)
        for first in (BQ + at, BK + at, BV + at):
            part = slice(first, first + TILE)
            copies.start("out", out_ref.at[:, part, :], out_hbm.at[:, part, :])
    copies.wait_all()


def settle_kernel(sums_ref, left_ref, right_ref, out_ref):
    out_ref[0] = sums_ref[0].astype(BF)
    for i in range(2):
        edges = jnp.concatenate([left_ref[i], right_ref[i]], 0).astype(F32)
        out_ref[1 + i] = (sums_ref[1 + i] + edges).astype(BF)


def join_kernel(
    group_ref, z0_hbm, z1_hbm, z2_hbm, z3_hbm, b_hbm, base_in, dq_out, dk_out, dv_out,
    a_ref, b_ref, base_ref, low_ref, sems,
):
    copies = Copies(sems)
    z = lax.rem(group_ref[0], SIDE)
    sets = ((dq_out, BQ), (dk_out, BK), (dv_out, BV))
    order = [SIDE] + list(range(SIDE))
    for block in order:
        at = slice(block * WIDE, block * WIDE + WIDE)
        if block == SIDE:
            for dz, share in enumerate((z0_hbm, z1_hbm, z2_hbm, z3_hbm)):
                copies.start(block, share, a_ref.at[dz])
        else:
            four = slice(SIDE * block, SIDE * block + SIDE)
            copies.start(block, b_hbm.at[four], b_ref.at[four])
        copies.start(block, base_in.at[:, :, at], base_ref.at[:, :, at])
    for block in order:
        copies.wait(block)
        at = slice(block * WIDE, block * WIDE + WIDE)
        for which, (out, row) in enumerate(sets):
            for j in range(SIDE):
                h = SIDE * block + j
                if block < SIDE:
                    more = b_ref[h, row : row + POS, :]
                else:
                    more = a_ref[lax.rem(j + SIDE - z, SIDE), row : row + POS, :]
                total = base_ref[which, :, cols(h)].astype(F32) + more.astype(F32)
                low_ref[which, :, cols(h)] = total.astype(BF)
            copies.start("out", low_ref.at[which, :, at], out.at[:, at])
    copies.wait_all()


VMEM = pl.BlockSpec(memory_space=pltpu.VMEM)
SMEM = pl.BlockSpec(memory_space=pltpu.SMEM)
ANY = pl.BlockSpec(memory_space=pl.ANY)
MIB = 1024 * 1024


def room(mib):
    return pltpu.CompilerParams(vmem_limit_bytes=mib * MIB)


SCRATCH = [
    pltpu.VMEM((KEYS, 2 * HEAD), BF),
    pltpu.VMEM((HEAD, KEYS), BF),
    pltpu.VMEM((KEYS, HEAD), F32),
    pltpu.VMEM((KEYS, HEAD), F32),
    pltpu.VMEM((2, 8, HEAD), F32),
]


def shape(*dims, dtype=BF):
    return jax.ShapeDtypeStruct(dims, dtype)


def cost(us):
    return pl.CostEstimate(flops=0, bytes_accessed=int(us * 3_000_000), transcendentals=0)


def cost(us):
    return pl.CostEstimate(flops=0, bytes_accessed=int(us * 3_000_000), transcendentals=0)


def pack_a_call(*args):
    halo = shape(2, TILE, args[4].shape[1])
    return pl.pallas_call(
        pack_a_kernel,
        out_shape=(shape(ROWS_B, HEAD),) * SIDE + (halo, halo),
        in_specs=[SMEM] * 3 + [VMEM] + [ANY] * 5,
        out_specs=[ANY] * (SIDE + 2),
        scratch_shapes=[pltpu.VMEM((POS, WIDE), BF)] * 5
        + [
            pltpu.VMEM((SIDE, ROWS_B, HEAD), BF),
            pltpu.VMEM((2, *halo.shape), BF),
            pltpu.SemaphoreType.DMA((15,)),
        ],
        compiler_params=room(60),
        cost_estimate=cost(3),
        name="pack_a",
    )(*args)


def pack_b_call(*args):
    q = args[4]
    return pl.pallas_call(
        pack_b_kernel,
        out_shape=shape(GROUP, ROWS_B, HEAD),
        in_specs=[SMEM] * 3 + [VMEM] + [ANY] * 5,
        out_specs=ANY,
        scratch_shapes=[pltpu.VMEM(q.shape, BF)] * 5
        + [pltpu.VMEM((GROUP, ROWS_B, HEAD), BF), pltpu.SemaphoreType.DMA((24,))],
        compiler_params=room(63),
        cost_estimate=cost(4),
        name="pack_b",
    )(*args)


def four_call(kernel, rows, scratch, us, name, place, shares):
    return pl.pallas_call(
        kernel,
        out_shape=(rows,) * SIDE,
        in_specs=[SMEM] + [VMEM] * SIDE,
        out_specs=[VMEM] * SIDE,
        scratch_shapes=scratch,
        compiler_params=room(32),
        cost_estimate=cost(us),
        name=name,
    )(place, *shares)


def head_call(arrived):
    return pl.pallas_call(
        head_kernel,
        out_shape=shape(GROUP, BACK_B, HEAD),
        in_specs=[ANY],
        out_specs=ANY,
        scratch_shapes=[
            pltpu.VMEM((GROUP, ROWS_B, HEAD), BF),
            pltpu.VMEM((GROUP, BACK_B, HEAD), BF),
            pltpu.SemaphoreType.DMA((15,)),
        ]
        + SCRATCH,
        compiler_params=room(60),
        cost_estimate=cost(8),
        name="head",
    )(arrived)


def settle_call(sums, left, right):
    edge = pl.BlockSpec((2, TILE, WIDE), lambda i: (0, 0, i))
    rows = pl.BlockSpec((3, POS, WIDE), lambda i: (0, 0, i))
    return pl.pallas_call(
        settle_kernel,
        grid=(sums.shape[2] // WIDE,),
        out_shape=shape(*sums.shape),
        in_specs=[rows, edge, edge],
        out_specs=rows,
        compiler_params=room(63),
        cost_estimate=cost(4),
        name="settle",
    )(sums, left, right)


def join_call(group, shares, b, base):
    out = shape(*base.shape[1:])
    return pl.pallas_call(
        join_kernel,
        out_shape=(out,) * 3,
        in_specs=[SMEM] + [ANY] * (SIDE + 2),
        out_specs=[ANY] * 3,
        scratch_shapes=[pltpu.VMEM((SIDE, BACK_B, HEAD), BF)]
        + [pltpu.VMEM(x.shape, x.dtype) for x in (b, base, base)]
        + [pltpu.SemaphoreType.DMA((28,))],
        compiler_params=room(60),
        cost_estimate=cost(4),
        name="join",
    )(group, *shares, b, base)


def own_call(inner, inner_at, q, k, v, o, g, before, after, lse):
    feature = q.shape[1]
    rows = pl.BlockSpec((POS, WIDE), lambda i: (0, i))
    edge = pl.BlockSpec((2, TILE, WIDE), lambda i: (0, 0, i))
    whole = pl.BlockSpec(lse.shape, lambda i: (0, 0, 0))
    halo = shape(2, TILE, feature)
    return pl.pallas_call(
        functools.partial(own_kernel, inner),
        grid=(feature // WIDE,),
        out_shape=(shape(3, POS, feature, dtype=F32), halo, halo),
        in_specs=[SMEM] + [rows] * 5 + [edge, edge, whole],
        out_specs=[pl.BlockSpec((3, POS, WIDE), lambda i: (0, 0, i)), edge, edge],
        compiler_params=room(63),
        cost_estimate=cost(9),
        name="own",
    )(inner_at, q, k, v, o, g, before, after, lse)


def around(axis_step, shares):
    def partner(i, step):
        y, z = i // SIDE, i % SIDE
        return (y + step[0]) % SIDE * SIDE + (z + step[1]) % SIDE

    out = [shares[0], None, None, None]
    for d in (2, 1, 3):
        step = (d * axis_step[0], d * axis_step[1])
        out[d] = lax.ppermute(shares[d], "group", [(i, partner(i, step)) for i in range(GROUP)])
    return out


def body(query_rows, key_rows, value_rows, out_rows, grad_out, log_sum_exp, far_frames, far_blocks):
    rows = tuple(a[0] for a in (query_rows, key_rows, value_rows, out_rows, grad_out))
    lse = jnp.transpose(log_sum_exp, (1, 0, 2))
    inner = lax.axis_size("inner")
    inner_at = lax.axis_index("inner").astype(jnp.int32)
    group_at = lax.axis_index("group").astype(jnp.int32)
    up = [(i, i + 1) for i in range(inner - 1)]
    down = [(i + 1, i) for i in range(inner - 1)]
    group = group_at.reshape(1)
    facts = (group, far_frames[0], far_blocks[0], lse)

    *sends_z, first_rows, last_rows = pack_a_call(*facts, *rows)
    got_z = around((0, 1), sends_z)
    before = lax.ppermute(last_rows, "inner", up)
    after = lax.ppermute(first_rows, "inner", down)
    send_b = pack_b_call(*facts, *rows)
    send_b, got_z, before, after = lax.optimization_barrier((send_b, got_z, before, after))
    got_b = lax.all_to_all(send_b, "group", 0, 0, tiled=True)

    sends_y = four_call(split_kernel, shape(SIDE, ROWS_A, HEAD), [], 3, "split", group, got_z)
    got_y = around((1, 0), sends_y)
    sums, to_low, to_high = own_call(inner, inner_at.reshape(1), *rows, before, after, lse)
    got_y, to_low, to_high = lax.optimization_barrier((got_y, to_low, to_high))
    scratch = [pltpu.VMEM((GROUP, HALF, HEAD), BF)] * 2 + SCRATCH
    back_y = four_call(quarter_kernel, shape(SIDE, ROWS_R, HEAD), scratch, 3, "quarter", group, got_y)
    back_y, to_low, to_high = lax.optimization_barrier((back_y, to_low, to_high))
    home_y = around((-1, 0), back_y)
    from_right = lax.ppermute(to_low, "inner", down)
    from_left = lax.ppermute(to_high, "inner", up)
    scratch = [pltpu.VMEM((SIDE, 2, POS, HEAD), F32)]
    back_z = four_call(merge_kernel, shape(BACK_B, HEAD), scratch, 3, "merge", group, home_y)

    got_b, back_z = lax.optimization_barrier((got_b, back_z))
    home_z = around((0, -1), back_z)
    back_b, from_left, from_right = lax.optimization_barrier((head_call(got_b), from_left, from_right))
    home_b = lax.all_to_all(back_b, "group", 0, 0, tiled=True)
    base = settle_call(sums, from_left, from_right)
    return tuple(a[None] for a in join_call(group, home_z, home_b, base))


def solution(mesh):
    shard = P("group", "inner", None)
    return jax.shard_map(
        body,
        mesh=mesh,
        in_specs=(shard,) * 5 + (P("group", None, "inner"), shard, shard),
        out_specs=(shard,) * 3,
        check_vma=False,
    )
```

```python
import functools
import math

import jax
import jax.numpy as jnp
from jax import lax
from jax.experimental import pallas as pl
from jax.experimental.pallas import tpu as pltpu
from jax.sharding import PartitionSpec as P

BF = jnp.bfloat16
F32 = jnp.float32
HEAD = 128
TILE = 64
HALF = 32
BLOCK = 8
GROUP = 16
SIDE = 4
POS = 128
WIDE = SIDE * HEAD
LOG2E = math.log2(math.e)
SCALE = 1.0 / math.sqrt(HEAD)
BIG = 1e30

BQ, BK, BV, BG, BS, ROWS_B = 0, 128, 256, 384, 512, 528
BACK_B = 384
AK, AV, AQ, AG, AS, ROWS_A = 0, 64, 128, 160, 192, 208
RK, RV, RQ, ROWS_R = 0, 64, 128, 160


def nt(a, b):
    return lax.dot_general(a, b, (((1,), (1,)), ((), ())), preferred_element_type=F32)


def nn(a, b):
    return jnp.dot(a, b, preferred_element_type=F32)


def cols(h):
    return pl.ds(h * HEAD, HEAD)


def three_terms(x):
    hi = x.astype(BF).astype(F32)
    mid = (x - hi).astype(BF).astype(F32)
    low = ((x - hi) - mid).astype(BF).astype(F32)
    return hi, mid, low


class Copies:
    def __init__(self, sems):
        self.sems, self.used, self.open = sems, 0, {}

    def start(self, key, source, target):
        copy = pltpu.make_async_copy(source, target, self.sems.at[self.used])
        copy.start()
        self.used += 1
        self.open.setdefault(key, []).append(copy)

    def wait(self, key):
        for copy in self.open.pop(key, []):
            copy.wait()

    def wait_all(self):
        for key in list(self.open):
            self.wait(key)


class Copies:
    def __init__(self, sems):
        self.sems, self.used, self.open = sems, 0, {}

    def start(self, key, source, target):
        copy = pltpu.make_async_copy(source, target, self.sems.at[self.used])
        copy.start()
        self.used += 1
        self.open.setdefault(key, []).append(copy)

    def wait(self, key):
        for copy in self.open.pop(key, []):
            copy.wait()

    def wait_all(self):
        for key in list(self.open):
            self.wait(key)


def deltas(grads, outs):
    ones = jnp.ones((8, HEAD), BF)
    prod = jnp.concatenate([g.astype(F32) * o.astype(F32) for g, o in zip(grads, outs)], 0)
    hi = prod.astype(BF)
    lo = (prod - hi.astype(F32)).astype(BF)
    sums = nt(ones, hi) + nt(ones, lo)
    return [sums[0:1, j * HEAD : j * HEAD + HEAD] for j in range(len(grads))]


def pair_masks(frame, frames_ref, blocks_ref):
    code = lax.broadcasted_iota(jnp.int32, (1, HEAD), 1)
    masks = []
    for t in range(POS // TILE):
        hit = jnp.abs(code // BLOCK - frame) == 1
        for j in range(frames_ref.shape[1]):
            hit = hit | (code == frames_ref[t, j] * BLOCK + blocks_ref[t, j])
        masks.append(hit.astype(F32))
    return masks


def stat_rows(lse, delta, masks):
    sub = lax.broadcasted_iota(jnp.int32, (16, HEAD), 0)
    rows = jnp.zeros((16, HEAD), F32)
    for i, term in enumerate(list(three_terms(lse) + three_terms(delta)) + masks):
        rows = jnp.where(sub == i, term, rows)
    return rows


def pack_a_kernel(
    group_ref, frames_ref, blocks_ref, lse_ref, q_hbm, k_hbm, v_hbm, o_hbm, g_hbm,
    z0_hbm, z1_hbm, z2_hbm, z3_hbm, low_hbm, high_hbm,
    q_all, k_all, v_all, o_all, g_all, send_ref, edge_ref, sems,
):
    copies = Copies(sems)
    at = slice(SIDE * WIDE, SIDE * WIDE + WIDE)
    for source, target in zip((g_hbm, o_hbm, q_hbm, k_hbm, v_hbm), (g_all, o_all, q_all, k_all, v_all)):
        copies.start("in", source.at[:, at], target)
    for i, source in enumerate((k_hbm, v_hbm)):
        copies.start("edge", source.at[0:TILE, :], edge_ref.at[0, i])
        copies.start("edge", source.at[POS - TILE : POS, :], edge_ref.at[1, i])
    masks = pair_masks(group_ref[0], frames_ref, blocks_ref)
    copies.wait("in")
    rows = deltas([g_all[:, cols(j)] for j in range(SIDE)], [o_all[:, cols(j)] for j in range(SIDE)])
    for j in range(SIDE):
        send_ref[j, BQ : BQ + POS, :] = q_all[:, cols(j)]
        send_ref[j, BK : BK + POS, :] = k_all[:, cols(j)]
        send_ref[j, BV : BV + POS, :] = v_all[:, cols(j)]
        send_ref[j, BG : BG + POS, :] = g_all[:, cols(j)]
        send_ref[j, BS:ROWS_B, :] = stat_rows(lse_ref[GROUP + j], rows[j], masks).astype(BF)
    for dz, out in enumerate((z0_hbm, z1_hbm, z2_hbm, z3_hbm)):
        copies.start("out", send_ref.at[lax.rem(group_ref[0] + dz, SIDE)], out)
    copies.wait("edge")
    copies.start("out", edge_ref.at[0], low_hbm)
    copies.start("out", edge_ref.at[1], high_hbm)
    copies.wait_all()


def pack_b_kernel(
    group_ref, frames_ref, blocks_ref, lse_ref, q_hbm, k_hbm, v_hbm, o_hbm, g_hbm, send_hbm,
    q_all, k_all, v_all, o_all, g_all, send_ref, sems,
):
    copies = Copies(sems)
    pairs = ((g_hbm, g_all), (o_hbm, o_all), (q_hbm, q_all), (k_hbm, k_all), (v_hbm, v_all))
    for block in range(SIDE):
        at = slice(block * WIDE, block * WIDE + WIDE)
        for source, target in pairs:
            copies.start(block, source.at[:, at], target.at[:, at])
    masks = pair_masks(group_ref[0], frames_ref, blocks_ref)
    for block in range(SIDE):
        copies.wait(block)
        heads = [block * SIDE + j for j in range(SIDE)]
        rows = deltas([g_all[:, cols(h)] for h in heads], [o_all[:, cols(h)] for h in heads])
        for j, h in enumerate(heads):
            send_ref[h, BQ : BQ + POS, :] = q_all[:, cols(h)]
            send_ref[h, BK : BK + POS, :] = k_all[:, cols(h)]
            send_ref[h, BV : BV + POS, :] = v_all[:, cols(h)]
            send_ref[h, BG : BG + POS, :] = g_all[:, cols(h)]
            send_ref[h, BS:ROWS_B, :] = stat_rows(lse_ref[h], rows[j], masks).astype(BF)
        four = slice(block * SIDE, block * SIDE + SIDE)
        copies.start("out", send_ref.at[four], send_hbm.at[four])
    copies.wait_all()


def split_kernel(group_ref, *refs):
    ins, outs = refs[:SIDE], refs[SIDE:]
    lane = lax.broadcasted_iota(jnp.int32, (16, HEAD), 1)
    sub = lax.broadcasted_iota(jnp.int32, (16, HEAD), 0)
    for dz, got in enumerate(ins):
        stats = got[BS:ROWS_B, :].astype(F32)
        for dy, out in enumerate(outs):
            y = lax.rem(group_ref[0] // SIDE + dy, SIDE)
            tile = pl.multiple_of((y // 2) * TILE, TILE)
            half = pl.multiple_of(y * HALF, HALF)
            out[dz, AK : AK + TILE, :] = got[pl.ds(BK + tile, TILE), :]
            out[dz, AV : AV + TILE, :] = got[pl.ds(BV + tile, TILE), :]
            out[dz, AQ : AQ + HALF, :] = got[pl.ds(BQ + half, HALF), :]
            out[dz, AG : AG + HALF, :] = got[pl.ds(BG + half, HALF), :]
            turned = pltpu.roll(stats, lax.rem(dz * HALF + HEAD - half, HEAD), 1)
            inside = (lane >= dz * HALF) & (lane < dz * HALF + HALF)
            kept = jnp.where(sub < 6, jnp.where(inside, turned, 0.0), stats)
            out[dz, AS:ROWS_A, :] = kept.astype(BF)


def own_kernel(
    inner, at_ref, q_ref, k_ref, v_ref, o_ref, g_ref, before_ref, after_ref, lse_ref,
    sums_ref, low_ref, high_ref,
):
    step = pl.program_id(0)
    width = POS + 2 * TILE
    key = lax.broadcasted_iota(jnp.int32, (width, POS), 0)
    query = lax.broadcasted_iota(jnp.int32, (width, POS), 1)
    first = jnp.where(at_ref[0] > 0, 0, TILE)
    last = jnp.where(at_ref[0] < inner - 1, width, width - TILE)
    inside = (key >= query) & (key <= query + 2 * TILE) & (key >= first) & (key < last)
    rows = deltas([g_ref[:, cols(j)] for j in range(SIDE)], [o_ref[:, cols(j)] for j in range(SIDE)])
    for j in range(SIDE):
        q = q_ref[:, cols(j)]
        g = g_ref[:, cols(j)]
        k = jnp.concatenate([before_ref[0, :, cols(j)], k_ref[:, cols(j)], after_ref[0, :, cols(j)]], 0)
        v = jnp.concatenate([before_ref[1, :, cols(j)], v_ref[:, cols(j)], after_ref[1, :, cols(j)]], 0)
        lse = lse_ref[step * SIDE + j]
        p = jnp.exp2(nt(k, q) * (SCALE * LOG2E) - lse * LOG2E)
        p = jnp.where(inside, p, 0.0)
        ds = (p * (nt(v, g) - rows[j])).astype(BF)
        dv = nn(p.astype(BF), g)
        dk = nn(ds, q) * SCALE
        dq = lax.dot_general(ds, k, (((0,), (0,)), ((), ())), preferred_element_type=F32)
        sums_ref[0, :, cols(j)] = dq * SCALE
        sums_ref[1, :, cols(j)] = dk[TILE : TILE + POS]
        sums_ref[2, :, cols(j)] = dv[TILE : TILE + POS]
        low_ref[0, :, cols(j)] = dk[0:TILE].astype(BF)
        low_ref[1, :, cols(j)] = dv[0:TILE].astype(BF)
        high_ref[0, :, cols(j)] = dk[TILE + POS :].astype(BF)
        high_ref[1, :, cols(j)] = dv[TILE + POS :].astype(BF)


CHUNK = 512
KEYS = GROUP * TILE


def attend(span, queries, key_code, k, v, mask, rows, kx_ref, kt_ref, dk_ref, dv_ref, row_ref, put_dq):
    for s in range(2):
        row_ref[s] = rows[s]
    lane = lax.broadcasted_iota(jnp.int32, (KEYS, HEAD), 1)
    spread = (key_code == lane).astype(F32).astype(BF)
    padded = jnp.concatenate([mask.astype(F32), jnp.zeros((HEAD - GROUP, HEAD), F32)], 0)
    kx_ref[:, 0:HEAD] = k
    kx_ref[:, HEAD:] = ((nt(spread, padded.astype(BF)) - 1.0) * BIG).astype(BF)
    kt_ref[...] = k.astype(F32).T.astype(BF)
    count = CHUNK // span
    query = lax.broadcasted_iota(jnp.int32, (CHUNK, HEAD), 0) // span
    column = lax.broadcasted_iota(jnp.int32, (CHUNK, HEAD), 1)

    for c in range(GROUP * span // CHUNK):
        frames = pl.ds(c * count, count)
        q, g = queries(frames)
        choose = (column == query + c * count).astype(F32).astype(BF)
        qx = jnp.concatenate([q, choose], 1)
        lanes = CHUNK // HEAD
        lse, delta = (
            jnp.concatenate([row_ref[s, pl.ds(lanes * c + i, 1), :] for i in range(lanes)], 1) for s in range(2)
        )
        p = jnp.exp2(nt(kx_ref[...], qx) * (SCALE * LOG2E) - lse * LOG2E)
        ds = (p * (nt(v, g) - delta)).astype(BF)
        dv, dk = nn(p.astype(BF), g), nn(ds, q)
        dv_ref[...] = dv if c == 0 else dv_ref[...] + dv
        dk_ref[...] = dk if c == 0 else dk_ref[...] + dk
        put_dq(frames, (nn(kt_ref[...], ds) * SCALE).T.astype(BF).reshape(count, span, HEAD))


def added(stats, at):
    return (stats[:, at, :] + stats[:, at + 1, :]) + stats[:, at + 2, :]


def stacked(rows):
    rows = rows + [jnp.zeros((8 - len(rows), HEAD), F32)] if len(rows) < 8 else rows
    return jnp.concatenate(rows, 0)


def quarter_kernel(group_ref, *refs):
    ins, outs = refs[:SIDE], refs[SIDE : 2 * SIDE]
    q_ref, g_ref, kx_ref, kt_ref, dk_ref, dv_ref, row_ref = refs[2 * SIDE :]
    y, z = group_ref[0] // SIDE, lax.rem(group_ref[0], SIDE)
    stats = jnp.concatenate([got[:, AS:ROWS_A, :] for got in ins], 0).astype(F32)
    rows = []
    for s in range(2):
        full = added(stats, 3 * s)
        rows.append(
            stacked(
                [
                    (full[i : i + 1] + full[i + 1 : i + 2]) + (full[i + 2 : i + 3] + full[i + 3 : i + 4])
                    for i in range(0, GROUP, SIDE)
                ]
            )
        )
    mask = jnp.where(y >= 2, stats[:, 7, :], stats[:, 6, :])
    k = jnp.concatenate([got[:, AK : AK + TILE, :] for got in ins], 0)
    v = jnp.concatenate([got[:, AV : AV + TILE, :] for got in ins], 0)
    for i, got in enumerate(ins):
        q_ref[SIDE * i : SIDE * i + SIDE] = got[:, AQ : AQ + HALF, :]
        g_ref[SIDE * i : SIDE * i + SIDE] = got[:, AG : AG + HALF, :]
    row = lax.broadcasted_iota(jnp.int32, (KEYS, HEAD), 0)
    source_y = (y + SIDE - row // (SIDE * TILE)) % SIDE
    source_z = (z + SIDE - (row // TILE) % SIDE) % SIDE
    key_code = (source_y * SIDE + source_z) * BLOCK + (row % TILE) // BLOCK

    def queries(frames):
        return q_ref[frames].reshape(CHUNK, HEAD), g_ref[frames].reshape(CHUNK, HEAD)

    def put_dq(frames, dq):
        q_ref[frames] = dq

    attend(
        HALF, queries, key_code, k.reshape(KEYS, HEAD), v.reshape(KEYS, HEAD), mask, rows,
        kx_ref, kt_ref, dk_ref, dv_ref, row_ref, put_dq,
    )
    span = SIDE * TILE
    for i, out in enumerate(outs):
        dk = (dk_ref[i * span : i * span + span] * SCALE).astype(BF)
        dv = dv_ref[i * span : i * span + span].astype(BF)
        out[:, RK : RK + TILE, :] = dk.reshape(SIDE, TILE, HEAD)
        out[:, RV : RV + TILE, :] = dv.reshape(SIDE, TILE, HEAD)
        out[:, RQ : RQ + HALF, :] = q_ref[SIDE * i : SIDE * i + SIDE]


def merge_kernel(group_ref, *refs):
    ins, outs, sum_ref = refs[:SIDE], refs[SIDE : 2 * SIDE], refs[2 * SIDE]
    sum_ref[...] = jnp.zeros_like(sum_ref)
    for dy, got in enumerate(ins):
        y = lax.rem(group_ref[0] // SIDE + dy, SIDE)
        tile = pl.multiple_of((y // 2) * TILE, TILE)
        half = pl.multiple_of(y * HALF, HALF)
        for dz, out in enumerate(outs):
            out[pl.ds(BQ + half, HALF), :] = got[dz, RQ:ROWS_R, :]
            sum_ref[dz, 0, pl.ds(tile, TILE), :] += got[dz, RK : RK + TILE, :].astype(F32)
            sum_ref[dz, 1, pl.ds(tile, TILE), :] += got[dz, RV : RV + TILE, :].astype(F32)
    for dz, out in enumerate(outs):
        out[BK : BK + POS, :] = sum_ref[dz, 0].astype(BF)
        out[BV : BV + POS, :] = sum_ref[dz, 1].astype(BF)


def head_kernel(in_hbm, out_hbm, in_ref, out_ref, sems, *scratch):
    copies = Copies(sems)

    def fetch(key, first, count):
        copies.start(key, in_hbm.at[:, first : first + count, :], in_ref.at[:, first : first + count, :])

    fetch("stats", BS, ROWS_B - BS)
    for unit in range(2):
        for at in (BK, BV, BQ, BG):
            fetch(unit, at + unit * TILE, TILE)
    key_code = lax.broadcasted_iota(jnp.int32, (KEYS, HEAD), 0) // BLOCK
    lane = lax.broadcasted_iota(jnp.int32, (1, HEAD), 1)
    copies.wait("stats")
    stats = in_ref[:, BS:ROWS_B, :].astype(F32)
    for unit in range(2):
        at = unit * TILE
        rows = []
        for s in range(2):
            full = added(stats, 3 * s)
            turned = pltpu.roll(full, TILE, 1)
            left, right = (full, turned) if unit == 0 else (turned, full)
            rows.append(
                stacked(
                    [jnp.where(lane < TILE, left[i : i + 1], right[i + 1 : i + 2]) for i in range(0, GROUP, 2)]
                )
            )

        def queries(frames):
            q = in_ref[frames, BQ + at : BQ + at + TILE, :].reshape(CHUNK, HEAD)
            g = in_ref[frames, BG + at : BG + at + TILE, :].reshape(CHUNK, HEAD)
            return q, g

        def put_dq(frames, dq):
            out_ref[frames, BQ + at : BQ + at + TILE, :] = dq

        copies.wait(unit)
        attend(
            TILE, queries, key_code,
            in_ref[:, BK + at : BK + at + TILE, :].reshape(KEYS, HEAD),
            in_ref[:, BV + at : BV + at + TILE, :].reshape(KEYS, HEAD),
            stats[:, 6 + unit, :], rows, *scratch, put_dq,
        )
        dk_ref, dv_ref = scratch[2:4]
        dk = (dk_ref[...] * SCALE).astype(BF).reshape(GROUP, TILE, HEAD)
        out_ref[:, BK + at : BK + at + TILE, :] = dk
        out_ref[:, BV + at : BV + at + TILE, :] = dv_ref[...].astype(BF).reshape(GROUP, TILE, HEAD)
        for first in (BQ + at, BK + at, BV + at):
            part = slice(first, first + TILE)
            copies.start("out", out_ref.at[:, part, :], out_hbm.at[:, part, :])
    copies.wait_all()


def settle_kernel(sums_ref, left_ref, right_ref, out_ref):
    out_ref[0] = sums_ref[0].astype(BF)
    for i in range(2):
        edges = jnp.concatenate([left_ref[i], right_ref[i]], 0).astype(F32)
        out_ref[1 + i] = (sums_ref[1 + i] + edges).astype(BF)


def join_kernel(
    group_ref, z0_hbm, z1_hbm, z2_hbm, z3_hbm, b_hbm, base_in, dq_out, dk_out, dv_out,
    a_ref, b_ref, base_ref, low_ref, sems,
):
    copies = Copies(sems)
    z = lax.rem(group_ref[0], SIDE)
    sets = ((dq_out, BQ), (dk_out, BK), (dv_out, BV))
    order = [SIDE] + list(range(SIDE))
    for block in order:
        at = slice(block * WIDE, block * WIDE + WIDE)
        if block == SIDE:
            for dz, share in enumerate((z0_hbm, z1_hbm, z2_hbm, z3_hbm)):
                copies.start(block, share, a_ref.at[dz])
        else:
            four = slice(SIDE * block, SIDE * block + SIDE)
            copies.start(block, b_hbm.at[four], b_ref.at[four])
        copies.start(block, base_in.at[:, :, at], base_ref.at[:, :, at])
    for block in order:
        copies.wait(block)
        at = slice(block * WIDE, block * WIDE + WIDE)
        for which, (out, row) in enumerate(sets):
            for j in range(SIDE):
                h = SIDE * block + j
                if block < SIDE:
                    more = b_ref[h, row : row + POS, :]
                else:
                    more = a_ref[lax.rem(j + SIDE - z, SIDE), row : row + POS, :]
                total = base_ref[which, :, cols(h)].astype(F32) + more.astype(F32)
                low_ref[which, :, cols(h)] = total.astype(BF)
            copies.start("out", low_ref.at[which, :, at], out.at[:, at])
    copies.wait_all()


VMEM = pl.BlockSpec(memory_space=pltpu.VMEM)
SMEM = pl.BlockSpec(memory_space=pltpu.SMEM)
ANY = pl.BlockSpec(memory_space=pl.ANY)
MIB = 1024 * 1024


def room(mib):
    return pltpu.CompilerParams(vmem_limit_bytes=mib * MIB)


SCRATCH = [
    pltpu.VMEM((KEYS, 2 * HEAD), BF),
    pltpu.VMEM((HEAD, KEYS), BF),
    pltpu.VMEM((KEYS, HEAD), F32),
    pltpu.VMEM((KEYS, HEAD), F32),
    pltpu.VMEM((2, 8, HEAD), F32),
]


def shape(*dims, dtype=BF):
    return jax.ShapeDtypeStruct(dims, dtype)


def cost(us):
    return pl.CostEstimate(flops=0, bytes_accessed=int(us * 3_000_000), transcendentals=0)


def cost(us):
    return pl.CostEstimate(flops=0, bytes_accessed=int(us * 3_000_000), transcendentals=0)


def pack_a_call(*args):
    halo = shape(2, TILE, args[4].shape[1])
    return pl.pallas_call(
        pack_a_kernel,
        out_shape=(shape(ROWS_B, HEAD),) * SIDE + (halo, halo),
        in_specs=[SMEM] * 3 + [VMEM] + [ANY] * 5,
        out_specs=[ANY] * (SIDE + 2),
        scratch_shapes=[pltpu.VMEM((POS, WIDE), BF)] * 5
        + [
            pltpu.VMEM((SIDE, ROWS_B, HEAD), BF),
            pltpu.VMEM((2, *halo.shape), BF),
            pltpu.SemaphoreType.DMA((15,)),
        ],
        compiler_params=room(60),
        cost_estimate=cost(3),
        name="pack_a",
    )(*args)


def pack_b_call(*args):
    q = args[4]
    return pl.pallas_call(
        pack_b_kernel,
        out_shape=shape(GROUP, ROWS_B, HEAD),
        in_specs=[SMEM] * 3 + [VMEM] + [ANY] * 5,
        out_specs=ANY,
        scratch_shapes=[pltpu.VMEM(q.shape, BF)] * 5
        + [pltpu.VMEM((GROUP, ROWS_B, HEAD), BF), pltpu.SemaphoreType.DMA((24,))],
        compiler_params=room(63),
        cost_estimate=cost(4),
        name="pack_b",
    )(*args)


def four_call(kernel, rows, scratch, us, name, place, shares):
    return pl.pallas_call(
        kernel,
        out_shape=(rows,) * SIDE,
        in_specs=[SMEM] + [VMEM] * SIDE,
        out_specs=[VMEM] * SIDE,
        scratch_shapes=scratch,
        compiler_params=room(32),
        cost_estimate=cost(us),
        name=name,
    )(place, *shares)


def head_call(arrived):
    return pl.pallas_call(
        head_kernel,
        out_shape=shape(GROUP, BACK_B, HEAD),
        in_specs=[ANY],
        out_specs=ANY,
        scratch_shapes=[
            pltpu.VMEM((GROUP, ROWS_B, HEAD), BF),
            pltpu.VMEM((GROUP, BACK_B, HEAD), BF),
            pltpu.SemaphoreType.DMA((15,)),
        ]
        + SCRATCH,
        compiler_params=room(60),
        cost_estimate=cost(8),
        name="head",
    )(arrived)


def settle_call(sums, left, right):
    edge = pl.BlockSpec((2, TILE, WIDE), lambda i: (0, 0, i))
    rows = pl.BlockSpec((3, POS, WIDE), lambda i: (0, 0, i))
    return pl.pallas_call(
        settle_kernel,
        grid=(sums.shape[2] // WIDE,),
        out_shape=shape(*sums.shape),
        in_specs=[rows, edge, edge],
        out_specs=rows,
        compiler_params=room(63),
        cost_estimate=cost(4),
        name="settle",
    )(sums, left, right)


def join_call(group, shares, b, base):
    out = shape(*base.shape[1:])
    return pl.pallas_call(
        join_kernel,
        out_shape=(out,) * 3,
        in_specs=[SMEM] + [ANY] * (SIDE + 2),
        out_specs=[ANY] * 3,
        scratch_shapes=[pltpu.VMEM((SIDE, BACK_B, HEAD), BF)]
        + [pltpu.VMEM(x.shape, x.dtype) for x in (b, base, base)]
        + [pltpu.SemaphoreType.DMA((28,))],
        compiler_params=room(60),
        cost_estimate=cost(4),
        name="join",
    )(group, *shares, b, base)


def own_call(inner, inner_at, q, k, v, o, g, before, after, lse):
    feature = q.shape[1]
    rows = pl.BlockSpec((POS, WIDE), lambda i: (0, i))
    edge = pl.BlockSpec((2, TILE, WIDE), lambda i: (0, 0, i))
    whole = pl.BlockSpec(lse.shape, lambda i: (0, 0, 0))
    halo = shape(2, TILE, feature)
    return pl.pallas_call(
        functools.partial(own_kernel, inner),
        grid=(feature // WIDE,),
        out_shape=(shape(3, POS, feature, dtype=F32), halo, halo),
        in_specs=[SMEM] + [rows] * 5 + [edge, edge, whole],
        out_specs=[pl.BlockSpec((3, POS, WIDE), lambda i: (0, 0, i)), edge, edge],
        compiler_params=room(63),
        cost_estimate=cost(9),
        name="own",
    )(inner_at, q, k, v, o, g, before, after, lse)


def around(axis_step, shares):
    def partner(i, step):
        y, z = i // SIDE, i % SIDE
        return (y + step[0]) % SIDE * SIDE + (z + step[1]) % SIDE

    out = [shares[0], None, None, None]
    for d in (2, 1, 3):
        step = (d * axis_step[0], d * axis_step[1])
        out[d] = lax.ppermute(shares[d], "group", [(i, partner(i, step)) for i in range(GROUP)])
    return out


def body(query_rows, key_rows, value_rows, out_rows, grad_out, log_sum_exp, far_frames, far_blocks):
    rows = tuple(a[0] for a in (query_rows, key_rows, value_rows, out_rows, grad_out))
    lse = jnp.transpose(log_sum_exp, (1, 0, 2))
    inner = lax.axis_size("inner")
    inner_at = lax.axis_index("inner").astype(jnp.int32)
    group_at = lax.axis_index("group").astype(jnp.int32)
    up = [(i, i + 1) for i in range(inner - 1)]
    down = [(i + 1, i) for i in range(inner - 1)]
    group = group_at.reshape(1)
    facts = (group, far_frames[0], far_blocks[0], lse)

    *sends_z, first_rows, last_rows = pack_a_call(*facts, *rows)
    got_z = around((0, 1), sends_z)
    before = lax.ppermute(last_rows, "inner", up)
    after = lax.ppermute(first_rows, "inner", down)
    send_b = pack_b_call(*facts, *rows)
    send_b, got_z, before, after = lax.optimization_barrier((send_b, got_z, before, after))
    got_b = lax.all_to_all(send_b, "group", 0, 0, tiled=True)

    sends_y = four_call(split_kernel, shape(SIDE, ROWS_A, HEAD), [], 3, "split", group, got_z)
    got_y = around((1, 0), sends_y)
    sums, to_low, to_high = own_call(inner, inner_at.reshape(1), *rows, before, after, lse)
    got_y, to_low, to_high = lax.optimization_barrier((got_y, to_low, to_high))
    scratch = [pltpu.VMEM((GROUP, HALF, HEAD), BF)] * 2 + SCRATCH
    back_y = four_call(quarter_kernel, shape(SIDE, ROWS_R, HEAD), scratch, 3, "quarter", group, got_y)
    back_y, to_low, to_high = lax.optimization_barrier((back_y, to_low, to_high))
    home_y = around((-1, 0), back_y)
    from_right = lax.ppermute(to_low, "inner", down)
    from_left = lax.ppermute(to_high, "inner", up)
    scratch = [pltpu.VMEM((SIDE, 2, POS, HEAD), F32)]
    back_z = four_call(merge_kernel, shape(BACK_B, HEAD), scratch, 3, "merge", group, home_y)

    got_b, back_z = lax.optimization_barrier((got_b, back_z))
    home_z = around((0, -1), back_z)
    back_b, from_left, from_right = lax.optimization_barrier((head_call(got_b), from_left, from_right))
    home_b = lax.all_to_all(back_b, "group", 0, 0, tiled=True)
    base = settle_call(sums, from_left, from_right)
    return tuple(a[None] for a in join_call(group, home_z, home_b, base))


def solution(mesh):
    shard = P("group", "inner", None)
    return jax.shard_map(
        body,
        mesh=mesh,
        in_specs=(shard,) * 5 + (P("group", None, "inner"), shard, shard),
        out_specs=(shard,) * 3,
        check_vma=False,
    )
```
